32 devices in a mesh: grp: 2 (over y), row: 4 (over z), col: 4 (over x, core).
Axes of the slice: x: 2, y: 2, z: 4, core: 2. Of those that a mesh axis runs over, the one named last changes fastest.
Arguments:
- inputs: bfloat16 [1024, 8192], P('row', 'col'), may hold values from -6 to 6
- w_gate: bfloat16 [8192, 14336], P('col', 'row'), may hold values from -0.0625 to 0.0625
- w_up: bfloat16 [8192, 14336], P('col', 'row'), may hold values from -0.0625 to 0.0625
- w_down: bfloat16 [14336, 8192], P('row', 'col'), may hold values from -0.046875 to 0.046875
- query: bfloat16 [16384, 14336], P(('grp', 'col'), 'row'), parts along dimension 0, may hold values from -0.0625 to 0.0625
- curvature: float32 [2048, 8192], P('grp', 'col'), parts along dimension 0, may hold values from 0.5 to 16
Outputs:
- gnvp: float32 [16384, 14336], P(('grp', 'col'), 'row'), parts along dimension 0
The draws below stay inside these ranges and needn't reach their ends.
There are 2 independent parts, one for each index of `grp`. The reference program is written for one: setup_inputs(seed, part) draws one part's arguments, and reference() takes and returns one part's arrays. A program takes and returns all parts, laid end to end along the dimension named above; an argument that names none is the same for every part. Nothing has to cross between parts.
All inputs are finite; a program needn't handle non-finite values.
Results may differ from the reference program's by a relative error of at most 0.0043.
Values may be sent and summed in bfloat16 or wider, within the bound.
No kernel may reach another device: no remote copies, remote signals or barrier semaphores. Data moves between devices by JAX's collectives and lax.ppermute only.
A program may use at most 320 MiB of HBM per device.

```python
import math
import jax
import jax.numpy as jnp

D = 8192
FF = 14336
TOKENS = 1024


def level_of(own_key, dims, shards, least, largest):
    loudness, own = 1.0, jax.random.fold_in(own_key, 6)
    for axis_at, blocks in shards:
        draws = jnp.exp(jax.random.uniform(jax.random.fold_in(own, axis_at), (blocks,), jnp.float32, least / len(shards), largest / len(shards)))
        loudness = loudness * jnp.repeat(draws, dims[axis_at] // blocks).reshape([-1 if axis == axis_at else 1 for axis in range(len(dims))])
    return loudness


def scatter_about(rng, shape, spread, reach, pieces=(), held_as=jnp.bfloat16):
    result = jax.random.normal(rng, shape, jnp.float32) * spread
    if len(pieces) > 0:
        result = level_of(rng, shape, pieces, -0.22, 0.18) * result
    return jnp.clip(result, min=-reach, max=reach).astype(held_as)


def setup_inputs(seed: int = 0, part: int = 0) -> dict:
    key_list = jax.random.split(jax.random.key(seed), 7)
    part_keys = jax.random.split(jax.random.fold_in(key_list[6], part), 7)
    return {
        "inputs": scatter_about(key_list[0], (TOKENS, D), 1.0, 6.0, ((0, 4), (1, 4))),
        "w_gate": scatter_about(key_list[1], (D, FF), D ** -0.5, 0.0625, ((0, 4), (1, 4))),
        "w_up": scatter_about(key_list[2], (D, FF), D ** -0.5, 0.0625, ((0, 4), (1, 4))),
        "w_down": scatter_about(key_list[3], (FF, D), FF ** -0.5, 0.046875, ((0, 4), (1, 4))),
        "query": scatter_about(part_keys[4], (D, FF), D ** -0.5, 0.0625, ((0, 4), (1, 4))),
        "curvature": jnp.clip(jnp.exp(math.log(16.0) - 3.465736 * jax.random.uniform(part_keys[5], (TOKENS, D), jnp.float32) ** level_of(part_keys[5], (TOKENS, D), ((1, 4),), -0.2, 0.2)), 0.5, 16.0),
    }


def silu_slope(values):
    sigmas = jax.nn.sigmoid(values)
    return sigmas * (1.0 + values * (1.0 - sigmas))


def reference(inputs, w_gate, w_up, w_down, query, curvature):
    gate_out = jnp.dot(inputs, w_gate, preferred_element_type=jnp.float32)
    up_out = jnp.dot(inputs, w_up, preferred_element_type=jnp.float32)
    tangent = jnp.dot(inputs, query, preferred_element_type=jnp.float32)
    slopes = silu_slope(gate_out)
    hidden_tangent = (slopes * tangent * up_out).astype(jnp.bfloat16)
    out_tangent = jnp.dot(hidden_tangent, w_down, preferred_element_type=jnp.float32)
    scaled = (curvature * out_tangent).astype(jnp.bfloat16)
    hidden_bar = jnp.dot(scaled, w_down.T, preferred_element_type=jnp.float32)
    gate_bar = (hidden_bar * up_out * slopes).astype(jnp.bfloat16)
    return jnp.dot(inputs.T, gate_bar, preferred_element_type=jnp.float32) / TOKENS
```

```python
import functools

import jax
import jax.numpy as jnp
from jax import lax
from jax.experimental import pallas as pl
from jax.experimental.pallas import tpu as pltpu
from jax.sharding import PartitionSpec as P

F16_TOP = 32768.0
LEAST_TOP = 1e-30
GROUPS = 2


def matmul(left, right):
    return jnp.dot(left, right, preferred_element_type=jnp.float32)


def times_down(left, w_down):
    return lax.dot_general(
        left, w_down, (((1,), (1,)), ((), ())), preferred_element_type=jnp.float32
    )


def slot_masks(count):
    bits = count.bit_length() - 1
    assert 1 << bits == count
    return [sum(((s >> b) & 1) << (bits - 1 - b) for b in range(bits)) for s in range(count)]


def swap(values, axis, mask):
    count = lax.axis_size(axis)
    return lax.ppermute(values, axis, [(i, i ^ mask) for i in range(count)])


def shift(values, axis):
    count = lax.axis_size(axis)
    return lax.ppermute(values, axis, [(i, (i + 1) % count) for i in range(count)])


def send_16(values, move):
    top = jnp.maximum(jnp.max(jnp.abs(values), axis=-1, keepdims=True), LEAST_TOP)
    coded = (values * (F16_TOP / top)).astype(jnp.float16)
    unit = (top * (1.0 / F16_TOP)).reshape(top.shape[:-1])
    coded, unit = move(coded), move(unit)
    return coded.astype(jnp.float32) * unit[..., None]


def sum_over_col(part):
    count = lax.axis_size("col")
    mask = 1
    while mask < count:
        half = part.shape[0] // 2
        keep, give = part[:half], part[half:]
        if mask == 1:
            part = keep + swap(give, "col", mask)
        else:
            part = keep + send_16(give, lambda v: swap(v, "col", mask))
        mask *= 2
    return part


def gather_over_col(rows):
    mask = lax.axis_size("col") // 2
    while mask >= 1:
        rows = jnp.concatenate([rows, swap(rows, "col", mask)], axis=0)
        mask //= 2
    return rows


def last_kernel(scale, parts, *refs):
    turned, bars, out_ref = refs[:parts], refs[parts : 2 * parts], refs[2 * parts]
    height = out_ref.shape[0]
    step = 512 if height % 512 == 0 else height

    @pl.loop(0, height // step)
    def _(at):
        rows = pl.ds(pl.multiple_of(at * step, step), step)
        total = jnp.dot(turned[0][rows, :], bars[0][...], preferred_element_type=jnp.float32)
        for left, right in zip(turned[1:], bars[1:]):
            total += jnp.dot(left[rows, :], right[...], preferred_element_type=jnp.float32)
        out_ref[rows, :] = total * scale


def last_product(turned, bars, tokens):
    features, hidden = turned[0].shape[0], bars[0].shape[1]
    tile = 512 if hidden % 512 == 0 else hidden
    depth = sum(t.shape[1] for t in turned)
    return pl.pallas_call(
        functools.partial(last_kernel, 1.0 / tokens, len(turned)),
        grid=(hidden // tile,),
        out_shape=jax.ShapeDtypeStruct((features, hidden), jnp.float32),
        in_specs=[pl.BlockSpec(t.shape, lambda j: (0, 0)) for t in turned]
        + [pl.BlockSpec((b.shape[0], tile), lambda j: (0, j)) for b in bars],
        out_specs=pl.BlockSpec((features, tile), lambda j: (0, j)),
        compiler_params=pltpu.CompilerParams(vmem_limit_bytes=40 * 1024 * 1024),
        cost_estimate=pl.CostEstimate(
            flops=2 * features * hidden * depth,
            bytes_accessed=features * hidden * 4 + depth * (features + hidden) * 2,
            transcendentals=0,
        ),
    )(*turned, *bars)


def per_device(inputs, w_gate, w_up, w_down, query, curvature):
    ring, count = lax.axis_size("row"), lax.axis_size("col")
    assert lax.axis_size("grp") == 2
    shard, width = inputs.shape
    tokens = shard * ring
    rows = shard // 2 // count
    per_group = ring // GROUPS
    masks = slot_masks(count)
    place, grp, me = lax.axis_index("col"), lax.axis_index("grp"), lax.axis_index("row")

    def own_rows(array, start, half):
        begin = start + half * (shard // 2)
        return jnp.stack(
            [
                lax.dynamic_slice_in_dim(array, begin + (place ^ mask) * rows, rows, 0)
                for mask in masks
            ]
        )

    def ring_pieces(first):
        pieces = [first]
        for _ in range(ring - 1):
            pieces.append(shift(pieces[-1], "row"))
        return pieces

    def grouped(pieces):
        return [
            jnp.concatenate(pieces[j * per_group : (j + 1) * per_group], axis=1).reshape(
                count * per_group * rows, width
            )
            for j in range(GROUPS)
        ]

    first = ring_pieces(own_rows(inputs, 0, grp))
    second = [own_rows(inputs, 0, 1 - grp)] + [swap(piece, "grp", 1) for piece in first[1:]]
    acts = [grouped(first), grouped(second)]
    curv = [own_rows(curvature, me * shard, grp), own_rows(curvature, me * shard, 1 - grp)]

    def out_pieces(half, gains):
        pieces = []
        for j in range(GROUPS):
            tangent = sum_over_col(matmul(acts[half][j], query))
            hidden_tangent = (gains[j] * tangent).astype(jnp.bfloat16)
            part = matmul(gather_over_col(hidden_tangent), w_down)
            part = part.reshape(count, per_group, rows, width)
            pieces += [part[:, k] for k in range(per_group)]
        return pieces

    def scaled_groups(half, pieces):
        total = pieces[1 % ring]
        for k in range(2, ring + 1):
            total = send_16(total, lambda v: shift(v, "row")) + pieces[k % ring]
        return grouped(ring_pieces((curv[half] * total).astype(jnp.bfloat16)))

    gains = []
    for j in range(GROUPS):
        gate_out = sum_over_col(matmul(acts[0][j], w_gate))
        up_out = sum_over_col(matmul(acts[0][j], w_up))
        sigmas = jax.nn.sigmoid(gate_out)
        gains.append(sigmas * (1.0 + gate_out * (1.0 - sigmas)) * up_out)
    gains = [gains, [swap(gain, "grp", 1) for gain in gains]]

    bars = []
    for half in range(2):
        groups = scaled_groups(half, out_pieces(half, gains[half]))
        for j in range(GROUPS):
            back = sum_over_col(times_down(groups[j], w_down))
            bars.append(gather_over_col((back * gains[half][j]).astype(jnp.bfloat16)))
    turned = [act.T for half in range(2) for act in acts[half]]
    return last_product(turned, bars, tokens)


def solution(mesh):
    in_specs = (
        P("row", "col"),
        P("col", "row"),
        P("col", "row"),
        P("row", "col"),
        P(("grp", "col"), "row"),
        P("grp", "col"),
    )
    out_specs = P(("grp", "col"), "row")
    return jax.shard_map(
        per_device, mesh=mesh, in_specs=in_specs, out_specs=out_specs, check_vma=False
    )
```

```python
import functools

import jax
import jax.numpy as jnp
from jax import lax
from jax.experimental import pallas as pl
from jax.experimental.pallas import tpu as pltpu
from jax.sharding import PartitionSpec as P

TOP_BITS = 14
LEAST_TOP = 1e-30
LANES = 128
MIB = 1024 * 1024


def slot_masks(count):
    bits = count.bit_length() - 1
    assert 1 << bits == count
    return [sum(((s >> b) & 1) << (bits - 1 - b) for b in range(bits)) for s in range(count)]


def swap(values, axis, mask):
    count = lax.axis_size(axis)
    return lax.ppermute(values, axis, [(i, i ^ mask) for i in range(count)])


def shift(values, axis):
    count = lax.axis_size(axis)
    return lax.ppermute(values, axis, [(i, (i + 1) % count) for i in range(count)])


def scaled_rows(values):
    top = jnp.max(jnp.abs(values), axis=-1, keepdims=True)
    power = jnp.ceil(jnp.log2(jnp.maximum(top, LEAST_TOP)))
    return values * jnp.exp2(TOP_BITS - power), power


def coded(values):
    body, power = scaled_rows(values)
    marks = jnp.broadcast_to(power, (*values.shape[:-1], LANES))
    return jnp.concatenate([body, marks], axis=-1)


def decoded(code):
    width = code.shape[-1] - LANES
    unit = jnp.exp2(code[..., width : width + 1].astype(jnp.float32) - TOP_BITS)
    return code[..., :width].astype(jnp.float32) * unit


def tile_of(size, tile):
    return tile if size % tile == 0 else size


def params(mib):
    return pltpu.CompilerParams(vmem_limit_bytes=mib * MIB)


def cost(rows, depth, width, moved):
    return pl.CostEstimate(
        flops=2 * rows * depth * width, bytes_accessed=moved, transcendentals=0
    )


ANYWHERE = pl.BlockSpec(memory_space=pl.ANY)


def split_kernel(count, turned, x_ref, *refs):
    keep_ref, give_ref = refs[-2:]
    half = keep_ref.shape[1]
    contract = (((1,), (1,)), ((), ())) if turned else (((1,), (0,)), ((), ()))
    for at in range(count):
        part = lax.dot_general(
            x_ref[...], refs[at][...], contract, preferred_element_type=jnp.float32
        )
        keep_ref[at] = part[:half]
        give_ref[at] = part[half:]


def split_products(x, weights, after=(), turned=False):
    rows, depth = x.shape
    width = weights[0].shape[0 if turned else 1]
    count = len(weights)
    tile = tile_of(width, 512 if count == 1 else 256)
    spec = (
        pl.BlockSpec((tile, depth), lambda j: (j, 0))
        if turned
        else pl.BlockSpec((depth, tile), lambda j: (0, j))
    )
    out = pl.BlockSpec((count, rows // 2, tile), lambda j: (0, 0, j))
    extra = list(after)
    return pl.pallas_call(
        functools.partial(split_kernel, count, turned),
        grid=(width // tile,),
        out_shape=[jax.ShapeDtypeStruct((count, rows // 2, width), jnp.float32)] * 2,
        in_specs=[pl.BlockSpec(x.shape, lambda j: (0, 0))]
        + [spec] * count
        + [ANYWHERE] * len(extra),
        out_specs=[out, out],
        compiler_params=params(32),
        cost_estimate=cost(
            rows, depth, width * count, count * width * (depth * 2 + rows * 4) + rows * depth * 2
        ),
    )(x, *weights, *extra)


def fold_kernel(keep_ref, got_ref, own_ref, code_ref):
    rows, width = own_ref.shape[1:]
    own_ref[0] = keep_ref[0, :rows] + got_ref[0, :rows]
    body, power = scaled_rows(keep_ref[0, rows:] + got_ref[0, rows:])
    code_ref[0, :, :width] = body
    code_ref[0, :, width:] = jnp.broadcast_to(power, (rows, LANES))


def fold(keep, got):
    count, both, width = keep.shape
    rows = both // 2
    if width % LANES or rows % 8:
        total = keep + got
        return total[:, :rows], coded(total[:, rows:])
    taken = pl.BlockSpec((1, both, width), lambda i: (i, 0, 0))
    return pl.pallas_call(
        fold_kernel,
        grid=(count,),
        out_shape=[
            jax.ShapeDtypeStruct((count, rows, width), jnp.float32),
            jax.ShapeDtypeStruct((count, rows, width + LANES), jnp.float32),
        ],
        in_specs=[taken, taken],
        out_specs=[
            pl.BlockSpec((1, rows, width), lambda i: (i, 0, 0)),
            pl.BlockSpec((1, rows, width + LANES), lambda i: (i, 0, 0)),
        ],
        compiler_params=params(20),
        cost_estimate=cost(1, count * both, width, count * both * width * 12),
    )(keep, got)


def whole_kernel(parts, *refs):
    weight_ref, out_ref, held = refs[parts], refs[-2], refs[-1]

    @pl.when(pl.program_id(0) == 0)
    def _():
        at = 0
        for part in refs[:parts]:
            held[at : at + part.shape[0]] = part[...]
            at += part.shape[0]

    out_ref[...] = jnp.dot(held[...], weight_ref[...], preferred_element_type=jnp.float32)


def whole_product(parts, weight):
    rows = sum(part.shape[0] for part in parts)
    depth, width = weight.shape
    tile = tile_of(width, 256)
    return pl.pallas_call(
        functools.partial(whole_kernel, len(parts)),
        grid=(width // tile,),
        out_shape=jax.ShapeDtypeStruct((rows, width), jnp.float32),
        in_specs=[pl.BlockSpec(part.shape, lambda j: (0, 0)) for part in parts]
        + [pl.BlockSpec((depth, tile), lambda j: (0, j))],
        out_specs=pl.BlockSpec((rows, tile), lambda j: (0, j)),
        scratch_shapes=[pltpu.VMEM((rows, depth), jnp.bfloat16)],
        compiler_params=params(24),
        cost_estimate=cost(rows, depth, width, (depth * width + rows * depth) * 2 + rows * width * 4),
    )(*parts, weight)


def last_kernel(scale, parts, *refs):
    turned, bars = refs[:parts], refs[parts:-3]
    out_ref, left, right = refs[-3:]
    height = out_ref.shape[0]
    step = tile_of(height, 512)

    @pl.when(pl.program_id(0) == 0)
    def _():
        at = 0
        for part in turned:
            left[:, at : at + part.shape[1]] = part[...]
            at += part.shape[1]

    at = 0
    for part in bars:
        right[at : at + part.shape[0]] = part[...]
        at += part.shape[0]

    @pl.loop(0, height // step)
    def _(at):
        rows = pl.ds(pl.multiple_of(at * step, step), step)
        total = jnp.dot(left[rows, :], right[...], preferred_element_type=jnp.float32)
        out_ref[rows, :] = total * scale


def last_product(turned, bars, tokens):
    features, hidden = turned[0].shape[0], bars[0].shape[1]
    tile = tile_of(hidden, 512)
    return pl.pallas_call(
        functools.partial(last_kernel, 1.0 / tokens, len(turned)),
        grid=(hidden // tile,),
        out_shape=jax.ShapeDtypeStruct((features, hidden), jnp.float32),
        in_specs=[pl.BlockSpec(t.shape, lambda j: (0, 0)) for t in turned]
        + [pl.BlockSpec((b.shape[0], tile), lambda j: (0, j)) for b in bars],
        out_specs=pl.BlockSpec((features, tile), lambda j: (0, j)),
        scratch_shapes=[
            pltpu.VMEM((features, tokens), jnp.bfloat16),
            pltpu.VMEM((tokens, tile), jnp.bfloat16),
        ],
        compiler_params=params(36),
        cost_estimate=cost(
            features, tokens, hidden, features * hidden * 4 + tokens * (features + hidden) * 2
        ),
    )(*turned, *bars)


def per_device(inputs, w_gate, w_up, w_down, query, curvature):
    ring, count = lax.axis_size("row"), lax.axis_size("col")
    assert lax.axis_size("grp") == 2 and ring % 4 == 0
    shard, width = inputs.shape
    tokens = shard * ring
    rows = shard // 2 // count
    masks = slot_masks(count)
    place, grp, me = lax.axis_index("col"), lax.axis_index("grp"), lax.axis_index("row")

    def own_rows(array, start, half):
        begin = start + half * (shard // 2)
        return jnp.stack(
            [
                lax.dynamic_slice_in_dim(array, begin + (place ^ mask) * rows, rows, 0)
                for mask in masks
            ]
        )

    def joined(pieces):
        return jnp.concatenate(pieces, axis=1).reshape(-1, pieces[0].shape[-1])

    def spans(*cuts):
        ends = [cut * ring // 4 for cut in cuts]
        return [list(range(a, b)) for a, b in zip(ends, ends[1:])]

    steps = [spans(0, 1, 2, 4), spans(0, 2, 4)]
    halves = (grp, 1 - grp)

    acts = [[own_rows(inputs, 0, half)] for half in halves]
    for k in range(1, ring):
        acts[0].append(shift(acts[0][-1], "row"))
        acts[1].append(swap(acts[0][-1], "grp", 1))

    def sum_over_col(x, weights, after, turned=False):
        keep, give = split_products(x, weights, after, turned)
        own, code = fold(keep, swap(give, "col", 1))
        mark, mask = code, 2
        while True:
            own = own + decoded(swap(code.astype(jnp.float16), "col", mask))
            mask *= 2
            if mask >= count:
                return own, mark
            upper = own.shape[1] // 2
            own, code = own[:, :upper], coded(own[:, upper:])

    def gather_over_col(values):
        parts, mask = [values], count // 2
        while mask >= 1:
            block = parts[0] if len(parts) == 1 else jnp.concatenate(parts, axis=0)
            parts.append(swap(block, "col", mask))
            mask //= 2
        return parts

    gains = [[None] * ring, [None] * ring]
    sums = [None, None]
    scaled = [None, None]

    def hidden(half, step, own):
        if half == 0:
            gate_out, up_out = own[0], own[1]
            sigmas = jax.nn.sigmoid(gate_out)
            gain = sigmas * (1.0 + gate_out * (1.0 - sigmas)) * up_out
            other = swap(gain, "grp", 1)
            for i, k in enumerate(step):
                gains[0][k] = gain[i * rows : (i + 1) * rows]
                gains[1][k] = other[i * rows : (i + 1) * rows]
        else:
            gain = jnp.concatenate([gains[1][k] for k in step], axis=0)
        return (gain * own[-1]).astype(jnp.bfloat16)

    def add_to_ring(half, step, out):
        out = out.reshape(count, len(step), rows, width)
        for i, k in enumerate(step):
            if k == 0:
                sums[half] = out[:, i]
            else:
                moved = shift(coded(sums[half]).astype(jnp.float16), "row")
                sums[half] = decoded(moved) + out[:, i]
        if step[-1] == ring - 1:
            owner = (me + 1) % ring
            curv = own_rows(curvature, owner * shard, halves[half])
            scaled[half] = (curv * sums[half]).astype(jnp.bfloat16)

    order = [(0, 0), (0, 1), (1, 0), (0, 2), (1, 1)]
    after = []
    for half, at in order:
        step = steps[half][at]
        x = joined([acts[half][k] for k in step])
        weights = [w_gate, w_up, query] if half == 0 else [query]
        own, mark = sum_over_col(x, weights, after)
        after = [mark]
        out = whole_product(gather_over_col(hidden(half, step, own)), w_down)
        add_to_ring(half, step, out)

    turned, bars = [], []
    for half in range(2):
        arrivals = [(ring - 1 + k) % ring for k in range(ring)]
        pieces = [scaled[half]]
        for _ in range(ring - 1):
            pieces.append(shift(pieces[-1], "row"))
        for span in spans(0, 2, 4):
            step = [arrivals[i] for i in span]
            turned.append(joined([acts[half][k] for k in step]).T)
            x = joined([pieces[i] for i in span])
            own, mark = sum_over_col(x, [w_down], after, True)
            after = [mark, turned[-1]]
            gain = jnp.concatenate([gains[half][k] for k in step], axis=0)
            bars += gather_over_col((own[0] * gain).astype(jnp.bfloat16))
    return last_product(turned, bars, tokens)


def solution(mesh):
    in_specs = (
        P("row", "col"),
        P("col", "row"),
        P("col", "row"),
        P("row", "col"),
        P(("grp", "col"), "row"),
        P("grp", "col"),
    )
    out_specs = P(("grp", "col"), "row")
    return jax.shard_map(
        per_device, mesh=mesh, in_specs=in_specs, out_specs=out_specs, check_vma=False
    )
```

```python
import functools

import jax
import jax.numpy as jnp
from jax import lax
from jax.experimental import pallas as pl
from jax.experimental.pallas import tpu as pltpu
from jax.sharding import PartitionSpec as P

TOP_BITS = 14
LEAST_TOP = 1e-30
FACTORS = 4
LANES = 128
MIB = 1024 * 1024
A_CUTS = (0, 1, 2, 4)
ORDER = [(0, 0), (0, 1), (1, 0), (0, 2), (1, 1)]


def slot_masks(count):
    bits = count.bit_length() - 1
    assert 1 << bits == count
    return [sum(((s >> b) & 1) << (bits - 1 - b) for b in range(bits)) for s in range(count)]


def swap(values, axis, mask):
    count = lax.axis_size(axis)
    return lax.ppermute(values, axis, [(i, i ^ mask) for i in range(count)])


def shift(values, axis, by=1):
    count = lax.axis_size(axis)
    return lax.ppermute(values, axis, [(i, (i + by) % count) for i in range(count)])


def scaled_rows(values):
    top = jnp.max(jnp.abs(values), axis=-1, keepdims=True)
    power = jnp.ceil(jnp.log2(jnp.maximum(top, LEAST_TOP))) - TOP_BITS
    factors, left = [], power
    for _ in range(FACTORS):
        factors.append(jnp.clip(left, -14.0, 15.0))
        left = left - factors[-1]
    power = power - left
    return values * jnp.exp2(-power), [jnp.exp2(factor) for factor in factors]


def coded(values):
    body, factors = scaled_rows(values)
    width = LANES // FACTORS
    marks = [jnp.broadcast_to(f, (*values.shape[:-1], width)) for f in factors]
    return jnp.concatenate([body, *marks], axis=-1)


def decoded(code):
    width = code.shape[-1] - LANES
    values = code[..., :width].astype(jnp.float32)
    for i in range(FACTORS):
        at = width + i * (LANES // FACTORS)
        values = values * code[..., at : at + 1].astype(jnp.float32)
    return values


def tile_of(size, tile):
    return tile if size % tile == 0 else size


PARAMS = pltpu.CompilerParams(vmem_limit_bytes=58 * MIB)
ANYWHERE = pl.BlockSpec(memory_space=pl.ANY)


def cost(rows, depth, width, moved):
    return pl.CostEstimate(
        flops=2 * rows * depth * width, bytes_accessed=moved, transcendentals=0
    )


def fixed(array):
    return pl.BlockSpec(array.shape, lambda j: (0,) * array.ndim)


def split_kernel(pieces, count, turned, *refs):
    xs, weights = refs[:pieces], refs[pieces : pieces + count]
    keep_ref, give_ref, held = refs[-3:]
    rows = xs[0].shape[0]
    half = rows // 2

    @pl.when(pl.program_id(0) == 0)
    def _():
        for i in range(pieces):
            held[i * rows : (i + 1) * rows] = xs[i][...]

    contract = (((1,), (1,)), ((), ())) if turned else (((1,), (0,)), ((), ()))
    for at in range(count):
        part = lax.dot_general(
            held[...], weights[at][...], contract, preferred_element_type=jnp.float32
        )
        for i in range(pieces):
            to = slice(i * half, (i + 1) * half)
            keep_ref[at, to] = part[i * rows : i * rows + half]
            give_ref[at, to] = part[i * rows + half : (i + 1) * rows]


def split_products(xs, weights, after=(), turned=False):
    rows, depth = len(xs) * xs[0].shape[0], xs[0].shape[1]
    width = weights[0].shape[0 if turned else 1]
    count = len(weights)
    tile = tile_of(width, 512)
    spec = (
        pl.BlockSpec((tile, depth), lambda j: (j, 0))
        if turned
        else pl.BlockSpec((depth, tile), lambda j: (0, j))
    )
    out = pl.BlockSpec((count, rows // 2, tile), lambda j: (0, 0, j))
    return pl.pallas_call(
        functools.partial(split_kernel, len(xs), count, turned),
        grid=(width // tile,),
        out_shape=[jax.ShapeDtypeStruct((count, rows // 2, width), jnp.float32)] * 2,
        in_specs=[fixed(x) for x in xs] + [spec] * count + [ANYWHERE] * len(after),
        out_specs=[out, out],
        scratch_shapes=[pltpu.VMEM((rows, depth), jnp.bfloat16)],
        compiler_params=PARAMS,
        cost_estimate=cost(
            rows, depth, width * count, count * width * (depth * 2 + rows * 4) + rows * depth * 2
        ),
    )(*xs, *weights, *after)


def fold_kernel(pieces, code, keep_ref, got_ref, own_ref, code_ref):
    width = own_ref.shape[2]
    rows = own_ref.shape[1] // pieces
    for i in range(pieces):
        to, at = slice(i * rows, (i + 1) * rows), 2 * i * rows
        own_ref[0, to] = keep_ref[0, at : at + rows] + got_ref[0, at : at + rows]
        at += rows
        lower = keep_ref[0, at : at + rows] + got_ref[0, at : at + rows]
        if not code:
            code_ref[0, to] = lower.astype(jnp.bfloat16)
            continue
        body, factors = scaled_rows(lower)
        code_ref[0, to, :width] = body
        marks = jnp.concatenate(
            [jnp.broadcast_to(f, (rows, LANES // FACTORS)) for f in factors], axis=-1
        )
        code_ref[0, to, width:] = marks


def fold(keep, got, pieces, code):
    count, both, width = keep.shape
    rows = both // 2
    if width % LANES or rows // pieces % 16:
        total = (keep + got).reshape(count, pieces, 2, rows // pieces, width)
        own, lower = (total[:, :, i].reshape(count, rows, width) for i in range(2))
        return own, coded(lower) if code else lower.astype(jnp.bfloat16)
    taken = pl.BlockSpec((1, both, width), lambda i: (i, 0, 0))
    sent = jax.ShapeDtypeStruct(
        (count, rows, width + LANES if code else width), jnp.float32 if code else jnp.bfloat16
    )
    return pl.pallas_call(
        functools.partial(fold_kernel, pieces, code),
        grid=(count,),
        out_shape=[jax.ShapeDtypeStruct((count, rows, width), jnp.float32), sent],
        in_specs=[taken, taken],
        out_specs=[
            pl.BlockSpec((1, rows, width), lambda i: (i, 0, 0)),
            pl.BlockSpec((1, *sent.shape[1:]), lambda i: (i, 0, 0)),
        ],
        compiler_params=PARAMS,
        cost_estimate=cost(1, count * both, width, count * both * width * 12),
    )(keep, got)


def placed(parts, pieces):
    total = sum(part.shape[0] for part in parts)
    least = min(part.shape[0] for part in parts)
    slots, rows = total // least, least // pieces
    if rows % 16:
        whole = jnp.concatenate(parts, axis=0).reshape(slots, pieces, rows, -1)
        return [whole.swapaxes(0, 1).reshape(total, -1)], [[(0, 0, total)]]
    runs, slot = [], 0
    for part in parts:
        runs.append([])
        for at in range(part.shape[0] // least):
            for i in range(pieces):
                runs[-1].append((at * least + i * rows, (i * slots + slot) * rows, rows))
            slot += 1
    return parts, runs


def put(runs, refs, held, base=0):
    for part, ref in zip(runs, refs):
        for source, to, rows in part:
            held[base + to : base + to + rows] = ref[source : source + rows]


def out_kernel(runs, first, *refs):
    weight_ref, outs, held = refs[len(runs)], refs[len(runs) + 1 : -1], refs[-1]

    @pl.when(pl.program_id(0) == 0)
    def _():
        put(runs, refs, held)

    part = jnp.dot(held[...], weight_ref[...], preferred_element_type=jnp.float32)
    rows = outs[0].shape[0]
    for i, out_ref in enumerate(outs):
        out_ref[...] = part[i * rows : (i + 1) * rows].astype(out_ref.dtype)


def out_product(parts, weight, pieces, first):
    parts, runs = placed(parts, pieces)
    rows = sum(part.shape[0] for part in parts)
    depth, width = weight.shape
    tile = tile_of(width, 256)
    types = [jnp.float32 if first and i == 0 else jnp.bfloat16 for i in range(pieces)]
    return pl.pallas_call(
        functools.partial(out_kernel, runs, first),
        grid=(width // tile,),
        out_shape=[jax.ShapeDtypeStruct((rows // pieces, width), t) for t in types],
        in_specs=[fixed(part) for part in parts]
        + [pl.BlockSpec((depth, tile), lambda j: (0, j))],
        out_specs=[pl.BlockSpec((rows // pieces, tile), lambda j: (0, j))] * pieces,
        scratch_shapes=[pltpu.VMEM((rows, depth), jnp.bfloat16)],
        compiler_params=PARAMS,
        cost_estimate=cost(rows, depth, width, (depth * width + rows * (depth + width)) * 2),
    )(*parts, weight)


def last_kernel(scale, runs, bases, parts, *refs):
    turned, bars = refs[:parts], refs[parts:-3]
    out_ref, left, right = refs[-3:]
    height = out_ref.shape[0]
    step = tile_of(height, 512)

    @pl.when(pl.program_id(0) == 0)
    def _():
        at = 0
        for part in turned:
            left[:, at : at + part.shape[1]] = part[...]
            at += part.shape[1]

    at = 0
    for run, base in zip(runs, bases):
        put(run, bars[at : at + len(run)], right, base)
        at += len(run)

    @pl.loop(0, height // step)
    def _(at):
        rows = pl.ds(pl.multiple_of(at * step, step), step)
        total = jnp.dot(left[rows, :], right[...], preferred_element_type=jnp.float32)
        out_ref[rows, :] = total * scale


def last_product(turned, steps, tokens):
    bars, runs, bases, base = [], [], [], 0
    for parts, pieces in steps:
        parts, run = placed(parts, pieces)
        bars += parts
        runs.append(run)
        bases.append(base)
        base += sum(part.shape[0] for part in parts)
    features, hidden = turned[0].shape[0], bars[0].shape[1]
    tile = tile_of(hidden, 512)
    return pl.pallas_call(
        functools.partial(last_kernel, 1.0 / tokens, runs, bases, len(turned)),
        grid=(hidden // tile,),
        out_shape=jax.ShapeDtypeStruct((features, hidden), jnp.float32),
        in_specs=[fixed(t) for t in turned]
        + [pl.BlockSpec((b.shape[0], tile), lambda j: (0, j)) for b in bars],
        out_specs=pl.BlockSpec((features, tile), lambda j: (0, j)),
        scratch_shapes=[
            pltpu.VMEM((features, tokens), jnp.bfloat16),
            pltpu.VMEM((tokens, tile), jnp.bfloat16),
        ],
        compiler_params=PARAMS,
        cost_estimate=cost(
            features, tokens, hidden, features * hidden * 4 + tokens * (features + hidden) * 2
        ),
    )(*turned, *bars)


def per_device(inputs, w_gate, w_up, w_down, query, curvature):
    ring, count = lax.axis_size("row"), lax.axis_size("col")
    assert lax.axis_size("grp") == 2 and ring % 4 == 0 and count >= 4
    shard, width = inputs.shape
    tokens = shard * ring
    rows = shard // 2 // count
    masks = slot_masks(count)
    place, grp, me = lax.axis_index("col"), lax.axis_index("grp"), lax.axis_index("row")

    def own_rows(array, start, half):
        begin = start + half * (shard // 2)
        return jnp.concatenate(
            [
                lax.dynamic_slice_in_dim(array, begin + (place ^ mask) * rows, rows, 0)
                for mask in masks
            ]
        )

    def spans(*cuts):
        ends = [cut * ring // 4 for cut in cuts]
        return [list(range(a, b)) for a, b in zip(ends, ends[1:])]

    steps = [spans(*A_CUTS), spans(0, 2, 4)]
    halves = (grp, 1 - grp)

    acts = [[own_rows(inputs, 0, half)] for half in halves]
    for k in range(1, ring):
        acts[0].append(shift(acts[0][-1], "row"))
        acts[1].append(swap(acts[0][-1], "grp", 1))
    curvs = [own_rows(curvature, me * shard, half) for half in halves]

    def sum_over_col(xs, weights, after, code, turned=False):
        keep, give = split_products(xs, weights, after, turned)
        own, sent = fold(keep, swap(give, "col", 1), len(xs), code)
        mark, mask = sent, 2
        while True:
            if code:
                own = own + decoded(swap(sent.astype(jnp.float16), "col", mask))
            else:
                own = own + swap(sent, "col", mask).astype(jnp.float32)
            mask *= 2
            if mask >= count:
                return own, mark
            both = own.reshape(own.shape[0], len(xs), 2, -1, own.shape[2])
            own, sent = (both[:, :, i].reshape(own.shape[0], -1, own.shape[2]) for i in range(2))
            sent = coded(sent) if code else sent.astype(jnp.bfloat16)

    def gather_over_col(values):
        parts, mask = [values], count // 2
        while mask >= 1:
            block = parts[0] if len(parts) == 1 else jnp.concatenate(parts, axis=0)
            parts.append(swap(block, "col", mask))
            mask //= 2
        return parts

    gains = [[None] * ring, [None] * ring]

    def gain_of(half, step):
        kept = [gains[half][k] for k in step]
        return kept[0] if len(kept) == 1 else jnp.concatenate(kept, axis=0)

    def hidden(half, step, own):
        if half == 0:
            gate_out, up_out = own[0], own[1]
            sigmas = jax.nn.sigmoid(gate_out)
            gain = sigmas * (1.0 + gate_out * (1.0 - sigmas)) * up_out
            other = swap(gain, "grp", 1)
            for i, k in enumerate(step):
                gains[0][k] = gain[i * rows : (i + 1) * rows]
                gains[1][k] = other[i * rows : (i + 1) * rows]
        else:
            gain = gain_of(1, step)
        return (gain * own[-1]).astype(jnp.bfloat16)

    totals = [[None] * ring, [None] * ring]
    after = []
    for half, at in ORDER:
        step = steps[half][at]
        weights = [w_gate, w_up, query] if half == 0 else [query]
        xs = [acts[half][k] for k in step]
        own, mark = sum_over_col(xs, weights, after, True)
        after = [mark]
        parts = gather_over_col(hidden(half, step, own))
        outs = out_product(parts, w_down, len(step), step[0] == 0)
        for k, out in zip(step, outs):
            totals[half][k] = shift(out, "row", -k) if k else out

    turned, bars = [], []
    for half in range(2):
        total = totals[half][0]
        for k in range(1, ring):
            total = total + totals[half][k].astype(jnp.float32)
        pieces = [(curvs[half] * total).astype(jnp.bfloat16)]
        for _ in range(ring - 1):
            pieces.append(shift(pieces[-1], "row"))
        for step in spans(0, 2, 4):
            kept = [acts[half][k] for k in step]
            if kept[0].shape[0] % LANES:
                kept = [jnp.concatenate(kept, axis=0)]
            turned += [array.T for array in kept]
            xs = [pieces[k] for k in step]
            own, mark = sum_over_col(xs, [w_down], after, False, True)
            after = [mark] + turned[-len(kept) :]
            bar = (own[0] * gain_of(half, step)).astype(jnp.bfloat16)
            bars.append((gather_over_col(bar), len(step)))
    return last_product(turned, bars, tokens)


def solution(mesh):
    in_specs = (
        P("row", "col"),
        P("col", "row"),
        P("col", "row"),
        P("row", "col"),
        P(("grp", "col"), "row"),
        P("grp", "col"),
    )
    out_specs = P(("grp", "col"), "row")
    return jax.shard_map(
        per_device, mesh=mesh, in_specs=in_specs, out_specs=out_specs, check_vma=False
    )
```

```python
import functools

import jax
import jax.numpy as jnp
from jax import lax
from jax.experimental import pallas as pl
from jax.experimental.pallas import tpu as pltpu
from jax.sharding import PartitionSpec as P

TOP_BITS = 14
LEAST_TOP = 1e-30
FACTORS = 4
LANES = 128
GROUPS = 2


def matmul(left, right):
    return jnp.dot(left, right, preferred_element_type=jnp.float32)


def times_down(left, w_down):
    return lax.dot_general(
        left, w_down, (((1,), (1,)), ((), ())), preferred_element_type=jnp.float32
    )


def slot_masks(count):
    bits = count.bit_length() - 1
    assert 1 << bits == count
    return [sum(((s >> b) & 1) << (bits - 1 - b) for b in range(bits)) for s in range(count)]


def swap(values, axis, mask):
    count = lax.axis_size(axis)
    return lax.ppermute(values, axis, [(i, i ^ mask) for i in range(count)])


def shift(values, axis, by=1):
    count = lax.axis_size(axis)
    return lax.ppermute(values, axis, [(i, (i + by) % count) for i in range(count)])


def coded(values):
    top = jnp.max(jnp.abs(values), axis=-1, keepdims=True)
    power = jnp.ceil(jnp.log2(jnp.maximum(top, LEAST_TOP))) - TOP_BITS
    factors, left = [], power
    for _ in range(FACTORS):
        factors.append(jnp.clip(left, -14.0, 15.0))
        left = left - factors[-1]
    shape = (*values.shape[:-1], LANES // FACTORS)
    marks = [jnp.broadcast_to(jnp.exp2(factor), shape) for factor in factors]
    body = values * jnp.exp2(left - power)
    return jnp.concatenate([body, *marks], axis=-1).astype(jnp.float16)


def decoded(code):
    width = code.shape[-1] - LANES
    values = code[..., :width].astype(jnp.float32)
    for i in range(FACTORS):
        at = width + i * (LANES // FACTORS)
        values = values * code[..., at : at + 1].astype(jnp.float32)
    return values


def tie(values, after):
    return lax.optimization_barrier((values, *after))[0] if after else values


def last_kernel(scale, parts, *refs):
    turned, bars, out_ref = refs[:parts], refs[parts : 2 * parts], refs[2 * parts]
    height = out_ref.shape[0]
    step = 512 if height % 512 == 0 else height

    @pl.loop(0, height // step)
    def _(at):
        rows = pl.ds(pl.multiple_of(at * step, step), step)
        total = jnp.dot(turned[0][rows, :], bars[0][...], preferred_element_type=jnp.float32)
        for left, right in zip(turned[1:], bars[1:]):
            total += jnp.dot(left[rows, :], right[...], preferred_element_type=jnp.float32)
        out_ref[rows, :] = total * scale


def last_product(turned, bars, tokens):
    features, hidden = turned[0].shape[0], bars[0].shape[1]
    tile = 512 if hidden % 512 == 0 else hidden
    depth = sum(t.shape[1] for t in turned)
    return pl.pallas_call(
        functools.partial(last_kernel, 1.0 / tokens, len(turned)),
        grid=(hidden // tile,),
        out_shape=jax.ShapeDtypeStruct((features, hidden), jnp.float32),
        in_specs=[pl.BlockSpec(t.shape, lambda j: (0, 0)) for t in turned]
        + [pl.BlockSpec((b.shape[0], tile), lambda j: (0, j)) for b in bars],
        out_specs=pl.BlockSpec((features, tile), lambda j: (0, j)),
        compiler_params=pltpu.CompilerParams(vmem_limit_bytes=40 * 1024 * 1024),
        cost_estimate=pl.CostEstimate(
            flops=2 * features * hidden * depth,
            bytes_accessed=features * hidden * 4 + depth * (features + hidden) * 2,
            transcendentals=0,
        ),
    )(*turned, *bars)


def per_device(inputs, w_gate, w_up, w_down, query, curvature):
    ring, count = lax.axis_size("row"), lax.axis_size("col")
    assert lax.axis_size("grp") == 2 and ring % GROUPS == 0 and count >= 4
    shard, width = inputs.shape
    tokens = shard * ring
    rows = shard // 2 // count
    per_group = ring // GROUPS
    masks = slot_masks(count)
    place, grp, me = lax.axis_index("col"), lax.axis_index("grp"), lax.axis_index("row")

    def own_rows(array, start, half):
        begin = start + half * (shard // 2)
        return jnp.stack(
            [
                lax.dynamic_slice_in_dim(array, begin + (place ^ mask) * rows, rows, 0)
                for mask in masks
            ]
        )

    def joined(pieces, j):
        return jnp.concatenate(pieces[j * per_group : (j + 1) * per_group], axis=1).reshape(
            count * per_group * rows, width
        )

    halves = (grp, 1 - grp)
    acts = [[own_rows(inputs, 0, half)] for half in halves]
    for k in range(1, per_group):
        acts[0].append(shift(acts[0][-1], "row"))
        acts[1].append(swap(acts[0][-1], "grp", 1))

    def fetch(j, after):
        acts[0].append(shift(acts[0][-1], "row"))
        for _ in range(1, per_group):
            acts[0].append(shift(tie(acts[0][-1], after), "row"))
        for piece in acts[0][-per_group:]:
            acts[1].append(swap(tie(piece, after), "grp", 1))

    def sum_over_col(parts, code):
        part, mask, marks = None, 1, []
        while mask < count:
            if part is None:
                half = parts[0].shape[0] // 2
                marks.append(jnp.stack([p[half:] for p in parts]))
                got = swap(marks[-1], "col", mask)
                halves_of = [
                    jnp.stack([p[at : at + half // 2] for p in parts])
                    + got[:, at : at + half // 2]
                    for at in (0, half // 2)
                ]
            else:
                half = part.shape[1] // 2
                halves_of = [part[:, :half], part[:, half:]]
            part, give = halves_of
            mask *= 2
            marks.append(coded(give) if code else give.astype(jnp.bfloat16))
            got = swap(marks[-1], "col", mask)
            part = part + (decoded(got) if code else got.astype(jnp.float32))
            if mask * 2 >= count:
                return part, marks

    def gather_over_col(values):
        mask = count // 2
        while mask >= 1:
            values = jnp.concatenate([values, swap(values, "col", mask)], axis=0)
            mask //= 2
        return values

    gains = [[None] * GROUPS, [None] * GROUPS]
    totals = [[], []]

    def project(half, j, after):
        x = joined([tie(piece, after) for piece in acts[half]], j)
        weights = [w_gate, w_up, query] if half == 0 else [query]
        return sum_over_col([matmul(x, w) for w in weights], True)

    def hidden(half, j, own):
        if half == 0:
            gate_out, up_out = own[0], own[1]
            sigmas = jax.nn.sigmoid(gate_out)
            gains[0][j] = sigmas * (1.0 + gate_out * (1.0 - sigmas)) * up_out
            gains[1][j] = swap(gains[0][j], "grp", 1)
        return (gains[half][j] * own[-1]).astype(jnp.bfloat16)

    def out_pieces(half, j, values):
        out = matmul(gather_over_col(values), w_down).reshape(count, per_group, rows, width)
        for i in range(per_group):
            k = j * per_group + i
            piece = out[:, i]
            totals[half].append(shift(piece.astype(jnp.bfloat16), "row", -k) if k else piece)

    after = [[], []]
    for j in range(GROUPS):
        for half in range(2):
            own, marks = project(half, j, after[-2] if half == 0 else after[-1])
            if half == 0 and j + 1 < GROUPS:
                fetch(j + 1, marks[:1])
            after.append(marks[-1:] if half == 0 else marks[:1])
            out_pieces(half, j, hidden(half, j, own))

    turned, bars = [], []
    for half in range(2):
        total = totals[half][0]
        for moved in totals[half][1:]:
            total = total + moved.astype(jnp.float32)
        curv = own_rows(curvature, me * shard, halves[half])
        pieces = [(curv * total).astype(jnp.bfloat16)]
        for _ in range(ring - 1):
            pieces.append(shift(pieces[-1], "row"))
        for j in range(GROUPS):
            turned.append(joined([tie(piece, pieces[:1]) for piece in acts[half]], j).T)
            x = joined(pieces, j)
            own, _ = sum_over_col([times_down(x, w_down)], False)
            bars.append(gather_over_col((own[0] * gains[half][j]).astype(jnp.bfloat16)))
    return last_product(turned, bars, tokens)


def solution(mesh):
    in_specs = (
        P("row", "col"),
        P("col", "row"),
        P("col", "row"),
        P("row", "col"),
        P(("grp", "col"), "row"),
        P("grp", "col"),
    )
    out_specs = P(("grp", "col"), "row")
    return jax.shard_map(
        per_device, mesh=mesh, in_specs=in_specs, out_specs=out_specs, check_vma=False
    )
```

```python
import functools
import math

import jax
import jax.numpy as jnp
from jax import lax
from jax.experimental import pallas as pl
from jax.experimental.pallas import tpu as pltpu
from jax.sharding import PartitionSpec as P

TOP_BITS = 14
LEAST_TOP = 1e-30
FACTORS = 4
LANES = 128
GROUPS = 2


def matmul(left, right):
    return jnp.dot(left, right, preferred_element_type=jnp.float32)


def times_down(left, w_down):
    return lax.dot_general(
        left, w_down, (((1,), (1,)), ((), ())), preferred_element_type=jnp.float32
    )


def slot_masks(count):
    bits = count.bit_length() - 1
    assert 1 << bits == count
    return [sum(((s >> b) & 1) << (bits - 1 - b) for b in range(bits)) for s in range(count)]


def swap(values, axis, mask):
    count = lax.axis_size(axis)
    return lax.ppermute(values, axis, [(i, i ^ mask) for i in range(count)])


def shift(values, axis, by=1):
    count = lax.axis_size(axis)
    return lax.ppermute(values, axis, [(i, (i + by) % count) for i in range(count)])


def coded(values):
    top = jnp.max(jnp.abs(values), axis=-1, keepdims=True)
    power = jnp.ceil(jnp.log2(jnp.maximum(top, LEAST_TOP))) - TOP_BITS
    factors, left = [], power
    for _ in range(FACTORS):
        factors.append(jnp.clip(left, -14.0, 15.0))
        left = left - factors[-1]
    shape = (*values.shape[:-1], LANES // FACTORS)
    marks = [jnp.broadcast_to(jnp.exp2(factor), shape) for factor in factors]
    body = values * jnp.exp2(left - power)
    return jnp.concatenate([body, *marks], axis=-1).astype(jnp.float16)


def decoded(code):
    width = code.shape[-1] - LANES
    values = code[..., :width].astype(jnp.float32)
    for i in range(FACTORS):
        at = width + i * (LANES // FACTORS)
        values = values * code[..., at : at + 1].astype(jnp.float32)
    return values


def tie(values, after):
    return lax.optimization_barrier((values, *after))[0] if after else values


def last_kernel(scale, parts, *refs):
    turned, bars, out_ref = refs[:parts], refs[parts : 2 * parts], refs[2 * parts]
    height = out_ref.shape[0]
    step = 512 if height % 512 == 0 else height

    @pl.loop(0, height // step)
    def _(at):
        rows = pl.ds(pl.multiple_of(at * step, step), step)
        total = jnp.dot(turned[0][rows, :], bars[0][...], preferred_element_type=jnp.float32)
        for left, right in zip(turned[1:], bars[1:]):
            total += jnp.dot(left[rows, :], right[...], preferred_element_type=jnp.float32)
        out_ref[rows, :] = total * scale


def last_product(turned, bars, tokens):
    features, hidden = turned[0].shape[0], bars[0].shape[1]
    tile = 512 if hidden % 512 == 0 else hidden
    depth = sum(t.shape[1] for t in turned)
    return pl.pallas_call(
        functools.partial(last_kernel, 1.0 / tokens, len(turned)),
        grid=(hidden // tile,),
        out_shape=jax.ShapeDtypeStruct((features, hidden), jnp.float32),
        in_specs=[pl.BlockSpec(t.shape, lambda j: (0, 0)) for t in turned]
        + [pl.BlockSpec((b.shape[0], tile), lambda j: (0, j)) for b in bars],
        out_specs=pl.BlockSpec((features, tile), lambda j: (0, j)),
        compiler_params=pltpu.CompilerParams(vmem_limit_bytes=40 * 1024 * 1024),
        cost_estimate=pl.CostEstimate(
            flops=2 * features * hidden * depth,
            bytes_accessed=features * hidden * 4 + depth * (features + hidden) * 2,
            transcendentals=0,
        ),
    )(*turned, *bars)


def per_device(inputs, w_gate, w_up, w_down, query, curvature):
    ring, count = lax.axis_size("row"), lax.axis_size("col")
    assert lax.axis_size("grp") == 2 and ring % GROUPS == 0 and count >= 4
    shard, width = inputs.shape
    tokens = shard * ring
    rows = shard // 2 // count
    per_group = ring // GROUPS
    masks = slot_masks(count)
    place, grp, me = lax.axis_index("col"), lax.axis_index("grp"), lax.axis_index("row")

    def own_rows(array, start, half):
        begin = start + half * (shard // 2)
        return jnp.stack(
            [
                lax.dynamic_slice_in_dim(array, begin + (place ^ mask) * rows, rows, 0)
                for mask in masks
            ]
        )

    def joined(pieces, j):
        return jnp.concatenate(pieces[j * per_group : (j + 1) * per_group], axis=1).reshape(
            count * per_group * rows, width
        )

    halves = (grp, 1 - grp)
    acts = [[None] * ring, [None] * ring]
    for half in range(2):
        acts[half][0] = own_rows(inputs, 0, halves[half])

    def fetch(step, after):
        for k in step:
            if k:
                acts[0][k] = shift(tie(acts[0][0], after), "row", k)

    def fetch_other(step, after):
        for k in step:
            if k:
                acts[1][k] = swap(tie(acts[0][k], after), "grp", 1)

    gate_scale = 2.0 ** math.floor(math.log2(65504.0 / (0.375 * width * count)))

    def pack(values, form):
        if form == "gate":
            return (values * gate_scale).astype(jnp.float16)
        return coded(values) if form == "up" else values.astype(jnp.bfloat16)

    def unpack(values, form):
        if form == "up":
            return decoded(values)
        values = values.astype(jnp.float32)
        return values * (1.0 / gate_scale) if form == "gate" else values

    def sum_over_col(part, form):
        half = part.shape[0] // 2
        got = swap(part[half:], "col", 1)
        cut = half // 2
        own, give = part[:cut] + got[:cut], part[cut:half] + got[cut:]
        mask, mark = 2, None
        while True:
            sent = pack(give, form)
            mark = sent if mark is None else mark
            own = own + unpack(swap(sent, "col", mask), form)
            mask *= 2
            if mask >= count:
                return own, mark
            cut = own.shape[0] // 2
            own, give = own[:cut], own[cut:]

    def gather_over_col(values):
        mask = count // 2
        while mask >= 1:
            values = jnp.concatenate([values, swap(values, "col", mask)], axis=0)
            mask //= 2
        return values

    steps = [list(range(j * per_group, (j + 1) * per_group)) for j in range(GROUPS)]
    fetch(steps[0], [])
    first = acts[0][1:per_group]
    for step in steps[1:]:
        fetch(step, first)
    fetch_other(steps[0], [])

    sums, marks = {}, []
    for half in range(2):
        for j in range(GROUPS):
            x = None
            for form in ("gate", "up", "tangent") if half == 0 else ("tangent",):
                after = marks[-2:-1]
                if x is None:
                    x = joined([p if p is None else tie(p, after) for p in acts[half]], j)
                else:
                    x = tie(x, after)
                weight = {"gate": w_gate, "up": w_up, "tangent": query}[form]
                sums[half, j, form], mark = sum_over_col(matmul(x, weight), form)
                marks.append(mark)
            if half == 0 and j + 1 < GROUPS:
                fetch_other(steps[j + 1], marks[-1:])

    gains = [[None] * GROUPS, [None] * GROUPS]
    for j in range(GROUPS):
        gate_out, up_out = sums[0, j, "gate"], sums[0, j, "up"]
        sigmas = jax.nn.sigmoid(gate_out)
        gains[0][j] = sigmas * (1.0 + gate_out * (1.0 - sigmas)) * up_out
        gains[1][j] = swap(gains[0][j], "grp", 1)

    last = ring - 1
    turned, bars = [], []
    for half in range(2):
        moved = []
        for j in range(GROUPS):
            hidden = (gains[half][j] * sums[half, j, "tangent"]).astype(jnp.bfloat16)
            out = matmul(gather_over_col(hidden), w_down).reshape(count, per_group, rows, width)
            for i, k in enumerate(steps[j]):
                piece = out[:, i]
                if k < last:
                    piece = shift(piece.astype(jnp.bfloat16), "row", last - k).astype(jnp.float32)
                moved.append(piece)
        total = moved[-1]
        for piece in moved[:-1]:
            total = total + piece
        curv = own_rows(curvature, (me + 1) % ring * shard, halves[half])
        pieces = [None] * last + [(curv * total).astype(jnp.bfloat16)]
        for k in reversed(range(last)):
            pieces[k] = shift(pieces[k + 1], "row", -1)
        for j in reversed(range(GROUPS)):
            after = pieces[last:]
            turned.append(joined([tie(piece, after) for piece in acts[half]], j).T)
            own, _ = sum_over_col(times_down(joined(pieces, j), w_down), "back")
            bars.append(gather_over_col((own * gains[half][j]).astype(jnp.bfloat16)))
    return last_product(turned, bars, tokens)


def solution(mesh):
    in_specs = (
        P("row", "col"),
        P("col", "row"),
        P("col", "row"),
        P("row", "col"),
        P(("grp", "col"), "row"),
        P("grp", "col"),
    )
    out_specs = P(("grp", "col"), "row")
    return jax.shard_map(
        per_device, mesh=mesh, in_specs=in_specs, out_specs=out_specs, check_vma=False
    )
```

```python
import functools
import math

import jax
import jax.numpy as jnp
from jax import lax
from jax.experimental import pallas as pl
from jax.experimental.pallas import tpu as pltpu
from jax.sharding import PartitionSpec as P

TOP_BITS = 14
LEAST_TOP = 1e-30
FACTORS = 4
LANES = 128
GROUPS = 2


def matmul(left, right):
    return jnp.dot(left, right, preferred_element_type=jnp.float32)


def times_down(left, w_down):
    return lax.dot_general(
        left, w_down, (((1,), (1,)), ((), ())), preferred_element_type=jnp.float32
    )


def slot_masks(count):
    bits = count.bit_length() - 1
    assert 1 << bits == count
    return [sum(((s >> b) & 1) << (bits - 1 - b) for b in range(bits)) for s in range(count)]


def swap(values, axis, mask):
    count = lax.axis_size(axis)
    return lax.ppermute(values, axis, [(i, i ^ mask) for i in range(count)])


def shift(values, axis, by=1):
    count = lax.axis_size(axis)
    return lax.ppermute(values, axis, [(i, (i + by) % count) for i in range(count)])


def coded(values):
    top = jnp.max(jnp.abs(values), axis=-1, keepdims=True)
    power = jnp.ceil(jnp.log2(jnp.maximum(top, LEAST_TOP))) - TOP_BITS
    factors, left = [], power
    for _ in range(FACTORS):
        factors.append(jnp.clip(left, -14.0, 15.0))
        left = left - factors[-1]
    shape = (*values.shape[:-1], LANES // FACTORS)
    marks = [jnp.broadcast_to(jnp.exp2(factor), shape) for factor in factors]
    body = values * jnp.exp2(left - power)
    return jnp.concatenate([body, *marks], axis=-1).astype(jnp.float16)


def decoded(code):
    width = code.shape[-1] - LANES
    values = code[..., :width].astype(jnp.float32)
    for i in range(FACTORS):
        at = width + i * (LANES // FACTORS)
        values = values * code[..., at : at + 1].astype(jnp.float32)
    return values


def tie(values, after):
    return lax.optimization_barrier((values, *after))[0] if after else values


def last_kernel(scale, parts, *refs):
    turned, bars, out_ref = refs[:parts], refs[parts : 2 * parts], refs[2 * parts]
    height = out_ref.shape[0]
    step = 512 if height % 512 == 0 else height

    @pl.loop(0, height // step)
    def _(at):
        rows = pl.ds(pl.multiple_of(at * step, step), step)
        total = jnp.dot(turned[0][rows, :], bars[0][...], preferred_element_type=jnp.float32)
        for left, right in zip(turned[1:], bars[1:]):
            total += jnp.dot(left[rows, :], right[...], preferred_element_type=jnp.float32)
        out_ref[rows, :] = total * scale


def last_product(turned, bars, tokens):
    features, hidden = turned[0].shape[0], bars[0].shape[1]
    tile = 512 if hidden % 512 == 0 else hidden
    depth = sum(t.shape[1] for t in turned)
    return pl.pallas_call(
        functools.partial(last_kernel, 1.0 / tokens, len(turned)),
        grid=(hidden // tile,),
        out_shape=jax.ShapeDtypeStruct((features, hidden), jnp.float32),
        in_specs=[pl.BlockSpec(t.shape, lambda j: (0, 0)) for t in turned]
        + [pl.BlockSpec((b.shape[0], tile), lambda j: (0, j)) for b in bars],
        out_specs=pl.BlockSpec((features, tile), lambda j: (0, j)),
        compiler_params=pltpu.CompilerParams(vmem_limit_bytes=40 * 1024 * 1024),
        cost_estimate=pl.CostEstimate(
            flops=2 * features * hidden * depth,
            bytes_accessed=features * hidden * 4 + depth * (features + hidden) * 2,
            transcendentals=0,
        ),
    )(*turned, *bars)


def per_device(inputs, w_gate, w_up, w_down, query, curvature):
    ring, count = lax.axis_size("row"), lax.axis_size("col")
    assert lax.axis_size("grp") == 2 and ring % GROUPS == 0 and count >= 4
    shard, width = inputs.shape
    tokens = shard * ring
    rows = shard // 2 // count
    per_group = ring // GROUPS
    masks = slot_masks(count)
    place, grp, me = lax.axis_index("col"), lax.axis_index("grp"), lax.axis_index("row")

    def own_rows(array, start, half):
        begin = start + half * (shard // 2)
        return jnp.stack(
            [
                lax.dynamic_slice_in_dim(array, begin + (place ^ mask) * rows, rows, 0)
                for mask in masks
            ]
        )

    def joined(pieces):
        return jnp.concatenate(pieces, axis=1).reshape(-1, pieces[0].shape[-1])

    halves = (grp, 1 - grp)
    own = [own_rows(inputs, 0, half) for half in halves]
    near = shift(own[0], "row")
    spread = [lax.all_gather(own[0], "row")]

    def piece_of(half, k):
        if k == 0:
            return own[half]
        if k == 1 and half == 0:
            return near
        return lax.dynamic_index_in_dim(spread[half], (me + ring - k) % ring, 0, keepdims=False)

    gate_scale = 2.0 ** math.floor(math.log2(65504.0 / (0.375 * width * count)))

    def pack(values, form):
        if form == "gate":
            return (values * gate_scale).astype(jnp.float16)
        return coded(values) if form == "up" else values.astype(jnp.bfloat16)

    def unpack(values, form):
        if form == "up":
            return decoded(values)
        values = values.astype(jnp.float32)
        return values * (1.0 / gate_scale) if form == "gate" else values

    def sum_over_col(part, form):
        half = part.shape[0] // 2
        first = part[half:]
        got = swap(first, "col", 1)
        cut = half // 2
        own, give = part[:cut] + got[:cut], part[cut:half] + got[cut:]
        mask, mark = 2, None
        while True:
            sent = pack(give, form)
            mark = sent if mark is None else mark
            own = own + unpack(swap(sent, "col", mask), form)
            mask *= 2
            if mask >= count:
                return own, mark, first
            cut = own.shape[0] // 2
            own, give = own[:cut], own[cut:]

    def gather_over_col(values):
        mask, mark = count // 2, None
        while mask >= 1:
            got = swap(values, "col", mask)
            mark = got if mark is None else mark
            values = jnp.concatenate([values, got], axis=0)
            mask //= 2
        return values, mark

    steps = [list(range(j * per_group, (j + 1) * per_group)) for j in range(GROUPS)]
    last = ring - 1
    sums, marks, xs = {}, [], {}
    gains = [[None] * GROUPS, [None] * GROUPS]
    moved = {}

    def project(half, j, form, after):
        after = after + [mark for mark, _ in marks[-2:-1]] + [total for _, total in marks[-3:-2]]
        if (half, j) in xs:
            x = tie(xs[half, j], after)
        else:
            xs[half, j] = x = joined([tie(piece_of(half, k), after) for k in steps[j]])
        weight = {"gate": w_gate, "up": w_up, "tangent": query}[form]
        sums[half, j, form], mark, start = sum_over_col(matmul(x, weight), form)
        marks.append((mark, sums[half, j, form]))
        return [start]

    def hidden_rows(half, j, after):
        if half == 0:
            gate_out, up_out = sums[0, j, "gate"], sums[0, j, "up"]
            sigmas = jax.nn.sigmoid(gate_out)
            gains[0][j] = sigmas * (1.0 + gate_out * (1.0 - sigmas)) * up_out
        tangent = tie(sums[half, j, "tangent"], after)
        hidden = (gains[half][j] * tangent).astype(jnp.bfloat16)
        return gather_over_col(hidden)

    def share_gain(j, after):
        both = lax.all_gather(tie(gains[0][j], after), "grp")
        gains[1][j] = lax.dynamic_index_in_dim(both, 1 - grp, 0, keepdims=False)

    def out_sums(half, j, hidden, after):
        out = matmul(tie(hidden, after), w_down).reshape(count, per_group, rows, width)
        for i, k in enumerate(steps[j]):
            piece = out[:, i]
            if k < last:
                piece = piece.astype(jnp.bfloat16)
                mark = piece
                piece = shift(piece, "row", last - k)
            moved[half, k] = piece
        return mark

    def scaled_pieces(half, after):
        total = moved[half, last]
        for k in range(last):
            total = total + tie(moved[half, k], after).astype(jnp.float32)
        curv = own_rows(curvature, (me + 1) % ring * shard, halves[half])
        pieces = [None] * last + [(curv * total).astype(jnp.bfloat16)]
        for k in reversed(range(last)):
            pieces[k] = shift(pieces[k + 1], "row", -1)
        return pieces

    turned, bars = [], []

    def back(half, j, pieces, after):
        x = joined([pieces[k] for k in steps[j]])
        turned.append(tie(xs[half, j], pieces[last:]).T)
        own, mark, _ = sum_over_col(times_down(tie(x, after), w_down), "back")
        bar = (own * gains[half][j]).astype(jnp.bfloat16)
        whole, near = gather_over_col(bar)
        bars.append(whole)
        return mark, bar, near

    tail = GROUPS - 1
    early = []
    for j in range(GROUPS):
        start = project(0, j, "up", [])
        if j:
            early.append(hidden_rows(0, j - 1, start))
        project(0, j, "gate", [])
        start = project(0, j, "tangent", [])
        if j == 0:
            spread.append(lax.all_gather(tie(own[1], spread + start), "row"))
        else:
            share_gain(j - 1, start)
    start = project(1, 0, "tangent", [near for _, near in early])
    ready = [out_sums(0, j, early[j][0], []) for j in range(tail)]
    hidden, _ = hidden_rows(0, tail, start)
    for j in range(1, GROUPS):
        start = project(1, j, "tangent", ready)
    share_gain(tail, start)
    ready = [out_sums(0, tail, hidden, [])]
    pieces = scaled_pieces(0, [])

    hidden = [hidden_rows(1, j, []) for j in range(GROUPS)]
    for j in range(tail):
        ready = [out_sums(1, j, hidden[j][0], ready)]
    mark, bar, near = back(0, tail, pieces, ready)
    out_sums(1, tail, hidden[tail][0], [mark])
    after = [mark]
    for j in reversed(range(tail)):
        mark, nextbar, nextnear = back(0, j, pieces, after)
        after = [mark, bar]
        bar, lastnear, near = nextbar, near, nextnear
    pieces = scaled_pieces(1, after)
    after = [lastnear, bar]
    for j in reversed(range(GROUPS)):
        mark, bar, nextnear = back(1, j, pieces, after)
        after, near = [mark, near], nextnear
    return last_product(turned, bars, tokens)


def solution(mesh):
    in_specs = (
        P("row", "col"),
        P("col", "row"),
        P("col", "row"),
        P("row", "col"),
        P(("grp", "col"), "row"),
        P("grp", "col"),
    )
    out_specs = P(("grp", "col"), "row")
    return jax.shard_map(
        per_device, mesh=mesh, in_specs=in_specs, out_specs=out_specs, check_vma=False
    )
```

```python
import functools
import math

import jax
import jax.numpy as jnp
from jax import lax
from jax.experimental import pallas as pl
from jax.experimental.pallas import tpu as pltpu
from jax.sharding import PartitionSpec as P

TOP_BITS = 14
LEAST_TOP = 1e-30
FACTORS = 4
LANES = 128
GROUPS = 2


def matmul(left, right):
    return jnp.dot(left, right, preferred_element_type=jnp.float32)


def times_down(left, w_down):
    return lax.dot_general(
        left, w_down, (((1,), (1,)), ((), ())), preferred_element_type=jnp.float32
    )


def slot_masks(count):
    bits = count.bit_length() - 1
    assert 1 << bits == count
    return [sum(((s >> b) & 1) << (bits - 1 - b) for b in range(bits)) for s in range(count)]


def swap(values, axis, mask):
    count = lax.axis_size(axis)
    return lax.ppermute(values, axis, [(i, i ^ mask) for i in range(count)])


def shift(values, axis, by=1):
    count = lax.axis_size(axis)
    return lax.ppermute(values, axis, [(i, (i + by) % count) for i in range(count)])


def coded(values):
    top = jnp.max(jnp.abs(values), axis=-1, keepdims=True)
    power = jnp.ceil(jnp.log2(jnp.maximum(top, LEAST_TOP))) - TOP_BITS
    factors, left = [], power
    for _ in range(FACTORS):
        factors.append(jnp.clip(left, -14.0, 15.0))
        left = left - factors[-1]
    shape = (*values.shape[:-1], LANES // FACTORS)
    marks = [jnp.broadcast_to(jnp.exp2(factor), shape) for factor in factors]
    body = values * jnp.exp2(left - power)
    return jnp.concatenate([body, *marks], axis=-1).astype(jnp.float16)


def decoded(code):
    width = code.shape[-1] - LANES
    values = code[..., :width].astype(jnp.float32)
    for i in range(FACTORS):
        at = width + i * (LANES // FACTORS)
        values = values * code[..., at : at + 1].astype(jnp.float32)
    return values


def tie(values, after):
    return lax.optimization_barrier((values, *after))[0] if after else values


def last_kernel(scale, parts, *refs):
    turned, bars, out_ref = refs[:parts], refs[parts : 2 * parts], refs[2 * parts]
    height = out_ref.shape[0]
    step = 512 if height % 512 == 0 else height

    @pl.loop(0, height // step)
    def _(at):
        rows = pl.ds(pl.multiple_of(at * step, step), step)
        total = jnp.dot(turned[0][rows, :], bars[0][...], preferred_element_type=jnp.float32)
        for left, right in zip(turned[1:], bars[1:]):
            total += jnp.dot(left[rows, :], right[...], preferred_element_type=jnp.float32)
        out_ref[rows, :] = total * scale


def last_product(turned, bars, tokens):
    features, hidden = turned[0].shape[0], bars[0].shape[1]
    tile = 512 if hidden % 512 == 0 else hidden
    depth = sum(t.shape[1] for t in turned)
    return pl.pallas_call(
        functools.partial(last_kernel, 1.0 / tokens, len(turned)),
        grid=(hidden // tile,),
        out_shape=jax.ShapeDtypeStruct((features, hidden), jnp.float32),
        in_specs=[pl.BlockSpec(t.shape, lambda j: (0, 0)) for t in turned]
        + [pl.BlockSpec((b.shape[0], tile), lambda j: (0, j)) for b in bars],
        out_specs=pl.BlockSpec((features, tile), lambda j: (0, j)),
        compiler_params=pltpu.CompilerParams(vmem_limit_bytes=40 * 1024 * 1024),
        cost_estimate=pl.CostEstimate(
            flops=2 * features * hidden * depth,
            bytes_accessed=features * hidden * 4 + depth * (features + hidden) * 2,
            transcendentals=0,
        ),
    )(*turned, *bars)


def per_device(inputs, w_gate, w_up, w_down, query, curvature):
    ring, count = lax.axis_size("row"), lax.axis_size("col")
    assert lax.axis_size("grp") == 2 and ring % GROUPS == 0 and count >= 4
    shard, width = inputs.shape
    tokens = shard * ring
    rows = shard // 2 // count
    per_group = ring // GROUPS
    masks = slot_masks(count)
    place, grp, me = lax.axis_index("col"), lax.axis_index("grp"), lax.axis_index("row")

    def own_rows(array, start, half):
        begin = start + half * (shard // 2)
        return jnp.stack(
            [
                lax.dynamic_slice_in_dim(array, begin + (place ^ mask) * rows, rows, 0)
                for mask in masks
            ]
        )

    def joined(pieces):
        return jnp.concatenate(pieces, axis=1).reshape(-1, pieces[0].shape[-1])

    halves = (grp, 1 - grp)
    own = [own_rows(inputs, 0, half) for half in halves]
    near = shift(own[0], "row")
    spread = [lax.all_gather(own[0], "row")]

    def piece_of(half, k):
        if k == 0:
            return own[half]
        if k == 1 and half == 0:
            return near
        return lax.dynamic_index_in_dim(spread[half], (me + ring - k) % ring, 0, keepdims=False)

    gate_scale = 2.0 ** math.floor(math.log2(65504.0 / (0.375 * width * count)))

    def pack(values, form):
        if form == "gate":
            return (values * gate_scale).astype(jnp.float16)
        return coded(values) if form == "up" else values.astype(jnp.bfloat16)

    def unpack(values, form):
        if form == "up":
            return decoded(values)
        values = values.astype(jnp.float32)
        return values * (1.0 / gate_scale) if form == "gate" else values

    def sum_over_col(part, form):
        half = part.shape[0] // 2
        first = part[half:]
        got = swap(first, "col", 1)
        cut = half // 2
        own, give = part[:cut] + got[:cut], part[cut:half] + got[cut:]
        mask, marks = 2, None
        while True:
            sent = pack(give, form)
            got = swap(sent, "col", mask)
            marks = marks or ([first], [sent], [got])
            own = own + unpack(got, form)
            mask *= 2
            if mask >= count:
                return own, *marks
            cut = own.shape[0] // 2
            own, give = own[:cut], own[cut:]

    def gather_over_col(values):
        mask, mark = count // 2, None
        while mask >= 1:
            got = swap(values, "col", mask)
            mark = got if mark is None else mark
            values = jnp.concatenate([values, got], axis=0)
            mask //= 2
        return values, mark

    steps = [list(range(j * per_group, (j + 1) * per_group)) for j in range(GROUPS)]
    last = ring - 1
    sums, marks, xs = {}, [], {}
    gains = [[None] * GROUPS, [None] * GROUPS]
    moved = {}

    def project(half, j, form, after):
        for sent in [mark[1] for mark in marks[-2:-1]] + [mark[2] for mark in marks[-3:-2]]:
            after = after + sent
        if (half, j) in xs:
            x = tie(xs[half, j], after)
        else:
            xs[half, j] = x = joined([tie(piece_of(half, k), after) for k in steps[j]])
        weight = {"gate": w_gate, "up": w_up, "tangent": query}[form]
        sums[half, j, form], *mark = sum_over_col(matmul(x, weight), form)
        marks.append(mark)
        return mark[0]

    def hidden_rows(half, j, after):
        if half == 0:
            gate_out, up_out = sums[0, j, "gate"], sums[0, j, "up"]
            sigmas = jax.nn.sigmoid(gate_out)
            gains[0][j] = sigmas * (1.0 + gate_out * (1.0 - sigmas)) * up_out
        tangent = tie(sums[half, j, "tangent"], after)
        hidden = (gains[half][j] * tangent).astype(jnp.bfloat16)
        return gather_over_col(hidden)

    def share_gain(j, after):
        both = lax.all_gather(tie(gains[0][j], after), "grp")
        gains[1][j] = lax.dynamic_index_in_dim(both, 1 - grp, 0, keepdims=False)

    def out_sums(half, j, hidden, after):
        out = matmul(tie(hidden, after), w_down).reshape(count, per_group, rows, width)
        for i, k in enumerate(steps[j]):
            piece = out[:, i]
            if k < last:
                piece = piece.astype(jnp.bfloat16)
                mark = piece
                piece = shift(piece, "row", last - k)
            moved[half, k] = piece
        return mark

    def scaled_pieces(half, after):
        total = moved[half, last]
        for k in range(last):
            total = total + tie(moved[half, k], after).astype(jnp.float32)
        curv = own_rows(curvature, (me + 1) % ring * shard, halves[half])
        pieces = [None] * last + [(curv * total).astype(jnp.bfloat16)]
        cut = ring // 4
        for k in reversed(range(cut, last)):
            pieces[k] = shift(pieces[k + 1], "row", -1)
        piece = tie(pieces[last], [pieces[steps[-1][0]]])
        for k in range(cut):
            pieces[k] = piece = shift(piece, "row")
        return pieces

    turned, bars = [], []

    def back(half, j, pieces, after):
        x = joined([tie(pieces[k], after) for k in steps[j]])
        turned.append(tie(xs[half, j], pieces[last:]).T)
        own, first, sent, got = sum_over_col(times_down(x, w_down), "back")
        whole, near = gather_over_col((own * gains[half][j]).astype(jnp.bfloat16))
        bars.append(whole)
        return first, sent, got, [near]

    tail = GROUPS - 1
    early = []
    for j in range(GROUPS):
        first = project(0, j, "up", [])
        if j:
            early.append(hidden_rows(0, j - 1, first))
        project(0, j, "gate", [])
        first = project(0, j, "tangent", [] if j else spread[:])
        if j == 0:
            spread.append(lax.all_gather(tie(own[1], spread + first), "row"))
        else:
            share_gain(j - 1, first)
    ready = [out_sums(0, j, early[j][0], marks[-2][1]) for j in range(tail)]
    first = project(1, 0, "tangent", ready)
    hidden, _ = hidden_rows(0, tail, first)
    for j in range(1, GROUPS):
        first = project(1, j, "tangent", [])
    share_gain(tail, first)
    ready = [out_sums(0, tail, hidden, [])]
    pieces = scaled_pieces(0, [])

    hidden = [hidden_rows(1, j, []) for j in range(GROUPS)]
    first, sent, got, near = back(0, tail, pieces, [])
    ready = [out_sums(1, j, hidden[j][0], first) for j in range(tail)]
    ready = [out_sums(1, tail, hidden[tail][0], ready + sent)]
    for j in reversed(range(tail)):
        _, sent, nextgot, nextnear = back(0, j, pieces, ready + got)
    pieces = scaled_pieces(1, sent + near)
    after = nextgot
    for j in reversed(range(GROUPS)):
        _, sent, _, near = back(1, j, pieces, after)
        after, nextnear = sent + nextnear, near
    return last_product(turned, bars, tokens)


def solution(mesh):
    in_specs = (
        P("row", "col"),
        P("col", "row"),
        P("col", "row"),
        P("row", "col"),
        P(("grp", "col"), "row"),
        P("grp", "col"),
    )
    out_specs = P(("grp", "col"), "row")
    return jax.shard_map(
        per_device, mesh=mesh, in_specs=in_specs, out_specs=out_specs, check_vma=False
    )
```

```python
import functools
import math

import jax
import jax.numpy as jnp
from jax import lax
from jax.experimental import pallas as pl
from jax.experimental.pallas import tpu as pltpu
from jax.sharding import PartitionSpec as P

TOP_BITS = 14
LEAST_TOP = 1e-30
FACTORS = 4
LANES = 128
GROUPS = 2


def matmul(left, right):
    return jnp.dot(left, right, preferred_element_type=jnp.float32)


def times_down(left, w_down):
    return lax.dot_general(
        left, w_down, (((1,), (1,)), ((), ())), preferred_element_type=jnp.float32
    )


def slot_masks(count):
    bits = count.bit_length() - 1
    assert 1 << bits == count
    return [sum(((s >> b) & 1) << (bits - 1 - b) for b in range(bits)) for s in range(count)]


def swap(values, axis, mask):
    count = lax.axis_size(axis)
    return lax.ppermute(values, axis, [(i, i ^ mask) for i in range(count)])


def shift(values, axis, by=1):
    count = lax.axis_size(axis)
    return lax.ppermute(values, axis, [(i, (i + by) % count) for i in range(count)])


def coded(values):
    top = jnp.max(jnp.abs(values), axis=-1, keepdims=True)
    power = jnp.ceil(jnp.log2(jnp.maximum(top, LEAST_TOP))) - TOP_BITS
    factors, left = [], power
    for _ in range(FACTORS):
        factors.append(jnp.clip(left, -14.0, 15.0))
        left = left - factors[-1]
    shape = (*values.shape[:-1], LANES // FACTORS)
    marks = [jnp.broadcast_to(jnp.exp2(factor), shape) for factor in factors]
    body = values * jnp.exp2(left - power)
    return jnp.concatenate([body, *marks], axis=-1).astype(jnp.float16)


def decoded(code):
    width = code.shape[-1] - LANES
    values = code[..., :width].astype(jnp.float32)
    for i in range(FACTORS):
        at = width + i * (LANES // FACTORS)
        values = values * code[..., at : at + 1].astype(jnp.float32)
    return values


def tie(values, after):
    return lax.optimization_barrier((values, *after))[0] if after else values


def last_kernel(scale, parts, *refs):
    turned, bars, out_ref = refs[:parts], refs[parts : 2 * parts], refs[2 * parts]
    height = out_ref.shape[0]
    step = 512 if height % 512 == 0 else height

    @pl.loop(0, height // step)
    def _(at):
        rows = pl.ds(pl.multiple_of(at * step, step), step)
        total = jnp.dot(turned[0][rows, :], bars[0][...], preferred_element_type=jnp.float32)
        for left, right in zip(turned[1:], bars[1:]):
            total += jnp.dot(left[rows, :], right[...], preferred_element_type=jnp.float32)
        out_ref[rows, :] = total * scale


def last_product(turned, bars, tokens):
    features, hidden = turned[0].shape[0], bars[0].shape[1]
    tile = 512 if hidden % 512 == 0 else hidden
    depth = sum(t.shape[1] for t in turned)
    return pl.pallas_call(
        functools.partial(last_kernel, 1.0 / tokens, len(turned)),
        grid=(hidden // tile,),
        out_shape=jax.ShapeDtypeStruct((features, hidden), jnp.float32),
        in_specs=[pl.BlockSpec(t.shape, lambda j: (0, 0)) for t in turned]
        + [pl.BlockSpec((b.shape[0], tile), lambda j: (0, j)) for b in bars],
        out_specs=pl.BlockSpec((features, tile), lambda j: (0, j)),
        compiler_params=pltpu.CompilerParams(vmem_limit_bytes=40 * 1024 * 1024),
        cost_estimate=pl.CostEstimate(
            flops=2 * features * hidden * depth,
            bytes_accessed=features * hidden * 4 + depth * (features + hidden) * 2,
            transcendentals=0,
        ),
    )(*turned, *bars)


def per_device(inputs, w_gate, w_up, w_down, query, curvature):
    ring, count = lax.axis_size("row"), lax.axis_size("col")
    assert lax.axis_size("grp") == 2 and ring % GROUPS == 0 and count >= 4
    shard, width = inputs.shape
    tokens = shard * ring
    rows = shard // 2 // count
    per_group = ring // GROUPS
    masks = slot_masks(count)
    place, grp, me = lax.axis_index("col"), lax.axis_index("grp"), lax.axis_index("row")

    def own_rows(array, start, half):
        begin = start + half * (shard // 2)
        return jnp.stack(
            [
                lax.dynamic_slice_in_dim(array, begin + (place ^ mask) * rows, rows, 0)
                for mask in masks
            ]
        )

    def joined(pieces):
        return jnp.concatenate(pieces, axis=1).reshape(-1, pieces[0].shape[-1])

    halves = (grp, 1 - grp)
    own = [own_rows(inputs, 0, half) for half in halves]
    fetched = {(0, 0): own[0], (1, 0): own[1]}
    for k in range(1, ring):
        needed = [fetched[0, i] for i in range(1, per_group)] if k >= per_group else []
        fetched[0, k] = shift(tie(own[0], needed), "row", k)

    def fetch_other(step, after):
        for k in step:
            if k:
                fetched[1, k] = swap(tie(fetched[0, k], after), "grp", 1)
        return [fetched[1, k] for k in step if k]

    gate_scale = 2.0 ** math.floor(math.log2(65504.0 / (0.375 * width * count)))

    def pack(values, form):
        if form == "gate":
            return (values * gate_scale).astype(jnp.float16)
        return coded(values) if form == "up" else values.astype(jnp.bfloat16)

    def unpack(values, form):
        if form == "up":
            return decoded(values)
        values = values.astype(jnp.float32)
        return values * (1.0 / gate_scale) if form == "gate" else values

    def sum_over_col(part, form):
        half = part.shape[0] // 2
        first = part[half:]
        got = swap(first, "col", 1)
        cut = half // 2
        own, give = part[:cut] + got[:cut], part[cut:half] + got[cut:]
        mask, marks = 2, None
        while True:
            sent = pack(give, form)
            got = swap(sent, "col", mask)
            marks = marks or ([first], [sent], [got])
            own = own + unpack(got, form)
            mask *= 2
            if mask >= count:
                return own, *marks
            cut = own.shape[0] // 2
            own, give = own[:cut], own[cut:]

    def gather_over_col(values):
        mask, mark = count // 2, None
        while mask >= 1:
            got = swap(values, "col", mask)
            mark = got if mark is None else mark
            values = jnp.concatenate([values, got], axis=0)
            mask //= 2
        return values, mark

    steps = [list(range(j * per_group, (j + 1) * per_group)) for j in range(GROUPS)]
    last = ring - 1
    sums, marks, xs = {}, [], {}
    gains = [[None] * GROUPS, [None] * GROUPS]
    moved = {}

    def project(half, j, form, after):
        for sent in [mark[1] for mark in marks[-2:-1]] + [mark[2] for mark in marks[-3:-2]]:
            after = after + sent
        if (half, j) in xs:
            x = tie(xs[half, j], after)
        else:
            xs[half, j] = x = joined([tie(fetched[half, k], after) for k in steps[j]])
        weight = {"gate": w_gate, "up": w_up, "tangent": query}[form]
        sums[half, j, form], *mark = sum_over_col(matmul(x, weight), form)
        marks.append(mark)
        return mark[0]

    def hidden_rows(half, j, after):
        if half == 0:
            gate_out, up_out = sums[0, j, "gate"], sums[0, j, "up"]
            sigmas = jax.nn.sigmoid(gate_out)
            gains[0][j] = sigmas * (1.0 + gate_out * (1.0 - sigmas)) * up_out
        tangent = tie(sums[half, j, "tangent"], after)
        hidden = (gains[half][j] * tangent).astype(jnp.bfloat16)
        return gather_over_col(hidden)

    def share_gain(j, after):
        both = lax.all_gather(tie(gains[0][j], after), "grp")
        gains[1][j] = lax.dynamic_index_in_dim(both, 1 - grp, 0, keepdims=False)

    def out_sums(half, j, hidden, after):
        out = matmul(tie(hidden, after), w_down).reshape(count, per_group, rows, width)
        for i, k in enumerate(steps[j]):
            piece = out[:, i]
            if k < last:
                piece = piece.astype(jnp.bfloat16)
                mark = piece
                piece = shift(piece, "row", last - k)
            moved[half, k] = piece
        return mark

    def scaled_pieces(half, after):
        total = moved[half, last]
        for k in range(last):
            total = total + tie(moved[half, k], after).astype(jnp.float32)
        curv = own_rows(curvature, (me + 1) % ring * shard, halves[half])
        pieces = [None] * last + [(curv * total).astype(jnp.bfloat16)]
        cut = ring // 4
        for k in reversed(range(cut, last)):
            pieces[k] = shift(pieces[k + 1], "row", -1)
        piece = tie(pieces[last], [pieces[steps[-1][0]]])
        for k in range(cut):
            pieces[k] = piece = shift(piece, "row")
        return pieces

    turned, bars = [], []

    def back(half, j, pieces, after):
        x = joined([tie(pieces[k], after) for k in steps[j]])
        turned.append(tie(xs[half, j], pieces[last:]).T)
        own, first, sent, got = sum_over_col(times_down(x, w_down), "back")
        whole, near = gather_over_col((own * gains[half][j]).astype(jnp.bfloat16))
        bars.append(whole)
        return first, sent, got, [near]

    tail = GROUPS - 1
    early, others = [], []
    for j in range(GROUPS):
        first = project(0, j, "up", [])
        if j:
            early.append(hidden_rows(0, j - 1, first))
        project(0, j, "gate", others[-1] if j == tail else [])
        first = project(0, j, "tangent", [])
        others.append(fetch_other(steps[j], first))
        if j:
            share_gain(j - 1, first)
    ready = [out_sums(0, j, early[j][0], marks[-2][1]) for j in range(tail)]
    first = project(1, 0, "tangent", ready)
    hidden, _ = hidden_rows(0, tail, first)
    for j in range(1, GROUPS):
        first = project(1, j, "tangent", others[j])
    share_gain(tail, first)
    ready = [out_sums(0, tail, hidden, [])]
    pieces = scaled_pieces(0, [])

    hidden = [hidden_rows(1, j, []) for j in range(GROUPS)]
    ready = [out_sums(1, j, hidden[j][0], []) for j in range(tail)]
    first, sent, got, near = back(0, tail, pieces, ready)
    ready = [out_sums(1, tail, hidden[tail][0], sent + [moved[1, 0]])]
    for j in reversed(range(tail)):
        come = [moved[1, k] for k in range(1, per_group)]
        _, sent, nextgot, _ = back(0, j, pieces, ready + got + come)
    pieces = scaled_pieces(1, sent + near)
    after = nextgot
    for j in reversed(range(GROUPS)):
        _, sent, got, near = back(1, j, pieces, after)
        after = got + near
    return last_product(turned, bars, tokens)


def solution(mesh):
    in_specs = (
        P("row", "col"),
        P("col", "row"),
        P("col", "row"),
        P("row", "col"),
        P(("grp", "col"), "row"),
        P("grp", "col"),
    )
    out_specs = P(("grp", "col"), "row")
    return jax.shard_map(
        per_device, mesh=mesh, in_specs=in_specs, out_specs=out_specs, check_vma=False
    )
```

```python
import functools
import math

import jax
import jax.numpy as jnp
from jax import lax
from jax.experimental import pallas as pl
from jax.experimental.pallas import tpu as pltpu
from jax.sharding import PartitionSpec as P

TOP_BITS = 14
LEAST_TOP = 1e-30
FACTORS = 4
LANES = 128
GROUPS = 2


def matmul(left, right):
    return jnp.dot(left, right, preferred_element_type=jnp.float32)


def times_down(left, w_down):
    return lax.dot_general(
        left, w_down, (((1,), (1,)), ((), ())), preferred_element_type=jnp.float32
    )


def slot_masks(count):
    bits = count.bit_length() - 1
    assert 1 << bits == count
    return [sum(((s >> b) & 1) << (bits - 1 - b) for b in range(bits)) for s in range(count)]


def swap(values, axis, mask):
    count = lax.axis_size(axis)
    return lax.ppermute(values, axis, [(i, i ^ mask) for i in range(count)])


def shift(values, axis, by=1):
    count = lax.axis_size(axis)
    return lax.ppermute(values, axis, [(i, (i + by) % count) for i in range(count)])


def coded(values):
    top = jnp.max(jnp.abs(values), axis=-1, keepdims=True)
    power = jnp.ceil(jnp.log2(jnp.maximum(top, LEAST_TOP))) - TOP_BITS
    factors, left = [], power
    for _ in range(FACTORS):
        factors.append(jnp.clip(left, -14.0, 15.0))
        left = left - factors[-1]
    shape = (*values.shape[:-1], LANES)
    at = lax.broadcasted_iota(jnp.int32, shape, len(shape) - 1) // (LANES // FACTORS)
    factor = factors[0]
    for i in range(1, FACTORS):
        factor = jnp.where(at == i, factors[i], factor)
    body = values * jnp.exp2(left - power)
    return jnp.concatenate([body, jnp.exp2(factor)], axis=-1).astype(jnp.float16)


def decoded(code):
    width = code.shape[-1] - LANES
    values = code[..., :width].astype(jnp.float32)
    for i in range(FACTORS):
        at = width + i * (LANES // FACTORS)
        values = values * code[..., at : at + 1].astype(jnp.float32)
    return values


def tie(values, after):
    return lax.optimization_barrier((values, *after))[0] if after else values


def last_kernel(scale, parts, *refs):
    turned, bars, out_ref = refs[:parts], refs[parts : 2 * parts], refs[2 * parts]
    height = out_ref.shape[0]
    step = 512 if height % 512 == 0 else height

    @pl.loop(0, height // step)
    def _(at):
        rows = pl.ds(pl.multiple_of(at * step, step), step)
        total = jnp.dot(turned[0][rows, :], bars[0][...], preferred_element_type=jnp.float32)
        for left, right in zip(turned[1:], bars[1:]):
            total += jnp.dot(left[rows, :], right[...], preferred_element_type=jnp.float32)
        out_ref[rows, :] = total * scale


def last_product(turned, bars, tokens):
    features, hidden = turned[0].shape[0], bars[0].shape[1]
    tile = 512 if hidden % 512 == 0 else hidden
    depth = sum(t.shape[1] for t in turned)
    return pl.pallas_call(
        functools.partial(last_kernel, 1.0 / tokens, len(turned)),
        grid=(hidden // tile,),
        out_shape=jax.ShapeDtypeStruct((features, hidden), jnp.float32),
        in_specs=[pl.BlockSpec(t.shape, lambda j: (0, 0)) for t in turned]
        + [pl.BlockSpec((b.shape[0], tile), lambda j: (0, j)) for b in bars],
        out_specs=pl.BlockSpec((features, tile), lambda j: (0, j)),
        compiler_params=pltpu.CompilerParams(vmem_limit_bytes=40 * 1024 * 1024),
        cost_estimate=pl.CostEstimate(
            flops=2 * features * hidden * depth,
            bytes_accessed=features * hidden * 4 + depth * (features + hidden) * 2,
            transcendentals=0,
        ),
    )(*turned, *bars)


def per_device(inputs, w_gate, w_up, w_down, query, curvature):
    ring, count = lax.axis_size("row"), lax.axis_size("col")
    assert lax.axis_size("grp") == 2 and ring % GROUPS == 0 and count >= 4
    shard, width = inputs.shape
    tokens = shard * ring
    rows = shard // 2 // count
    per_group = ring // GROUPS
    masks = slot_masks(count)
    place, grp, me = lax.axis_index("col"), lax.axis_index("grp"), lax.axis_index("row")

    def own_rows(array, start, half):
        begin = start + half * (shard // 2)
        return jnp.stack(
            [
                lax.dynamic_slice_in_dim(array, begin + (place ^ mask) * rows, rows, 0)
                for mask in masks
            ]
        )

    def joined(pieces):
        return jnp.concatenate(pieces, axis=1).reshape(-1, pieces[0].shape[-1])

    halves = (grp, 1 - grp)
    own = [own_rows(inputs, 0, half) for half in halves]
    fetched = {(0, 0): own[0], (1, 0): own[1]}
    for k in range(1, ring):
        fetched[0, k] = shift(own[0], "row", k)

    gate_scale = 2.0 ** math.floor(math.log2(65504.0 / (0.375 * width * count)))

    def pack(values, form):
        if form == "gate":
            return (values * gate_scale).astype(jnp.float16)
        return coded(values) if form == "up" else values.astype(jnp.bfloat16)

    def unpack(values, form):
        if form == "up":
            return decoded(values)
        values = values.astype(jnp.float32)
        return values * (1.0 / gate_scale) if form == "gate" else values

    def sum_over_col(part, form):
        half = part.shape[0] // 2
        first = part[half:]
        got = swap(first, "col", 1)
        cut = half // 2
        own, give = part[:cut] + got[:cut], part[cut:half] + got[cut:]
        mask, marks = 2, None
        while True:
            sent = pack(give, form)
            got = swap(sent, "col", mask)
            marks = marks or ([first], [sent], [got])
            own = own + unpack(got, form)
            mask *= 2
            if mask >= count:
                return own, *marks
            cut = own.shape[0] // 2
            own, give = own[:cut], own[cut:]

    def gather_over_col(values):
        mask, mark = count // 2, None
        while mask >= 1:
            got = swap(values, "col", mask)
            mark = got if mark is None else mark
            values = jnp.concatenate([values, got], axis=0)
            mask //= 2
        return values, mark

    last = ring - 1
    sums, marks, gains, moved = {}, [], {}, {}

    def project(half, x, form, after):
        for sent in [mark[1] for mark in marks[-2:-1]] + [mark[2] for mark in marks[-3:-2]]:
            after = after + sent
        weight = {"gate": w_gate, "up": w_up, "tangent": query}[form]
        sums[half, form], *mark = sum_over_col(matmul(tie(x, after), weight), form)
        marks.append(mark)
        return mark[0]

    def out_sums(half, early, late):
        hidden = (gains[half] * tie(sums[half, "tangent"], early)).astype(jnp.bfloat16)
        whole, _ = gather_over_col(hidden)
        out = matmul(tie(whole, late), w_down).reshape(count, ring, rows, width)
        sent = [out[:, k].astype(jnp.bfloat16) for k in range(last)]
        for k in range(last):
            moved[half, k] = shift(sent[k], "row", last - k)
        moved[half, last] = out[:, last]
        return sent

    def scaled_pieces(half):
        total = moved[half, last]
        for k in range(last):
            total = total + moved[half, k].astype(jnp.float32)
        curv = own_rows(curvature, (me + 1) % ring * shard, halves[half])
        pieces = [None] * last + [(curv * total).astype(jnp.bfloat16)]
        cut = ring // 4
        for k in reversed(range(cut, last)):
            pieces[k] = shift(pieces[k + 1], "row", -1)
        piece = tie(pieces[last], [pieces[ring - per_group]])
        for k in range(cut):
            pieces[k] = piece = shift(piece, "row")
        return pieces

    turned, bars = [], []

    def back(half, j, pieces, after):
        step = slice(j * per_group, (j + 1) * per_group)
        x = joined([tie(piece, after) for piece in pieces[step]])
        act = tie(xs[half], pieces[last:]).reshape(count, ring, rows, width)
        turned.append(act[:, step].reshape(-1, width).T)
        own, first, sent, got = sum_over_col(times_down(x, w_down), "back")
        gain = gains[half].reshape(ring, rows, -1)[step].reshape(own.shape)
        whole, near = gather_over_col((own * gain).astype(jnp.bfloat16))
        bars.append(whole)
        return first, sent, got, [near]

    xs = [joined([fetched[0, k] for k in range(ring)])]
    first = project(0, xs[0], "up", [])
    for k in range(1, ring):
        fetched[1, k] = swap(tie(fetched[0, k], first), "grp", 1)
    project(0, xs[0], "gate", [])
    project(0, xs[0], "tangent", [])
    xs.append(joined([tie(fetched[1, k], marks[-2][1]) for k in range(ring)]))
    first = project(1, xs[1], "tangent", [])

    gate_out = sums[0, "gate"]
    sigmas = jax.nn.sigmoid(gate_out)
    gains[0] = sigmas * (1.0 + gate_out * (1.0 - sigmas)) * sums[0, "up"]
    gains[1] = swap(gains[0], "grp", 1)
    out_sums(0, first, marks[-1][1])
    after = out_sums(1, [], [])
    pieces = scaled_pieces(0)
    near = []
    for j in reversed(range(GROUPS)):
        _, sent, got, nextnear = back(0, j, pieces, after)
        after, near = got + near, nextnear
    pieces = scaled_pieces(1)
    for j in reversed(range(GROUPS)):
        _, sent, got, nextnear = back(1, j, pieces, after)
        after, near = got + near, nextnear
    return last_product(turned, bars, tokens)


def solution(mesh):
    in_specs = (
        P("row", "col"),
        P("col", "row"),
        P("col", "row"),
        P("row", "col"),
        P(("grp", "col"), "row"),
        P("grp", "col"),
    )
    out_specs = P(("grp", "col"), "row")
    return jax.shard_map(
        per_device, mesh=mesh, in_specs=in_specs, out_specs=out_specs, check_vma=False
    )
```

```python
import functools
import math

import jax
import jax.numpy as jnp
from jax import lax
from jax.experimental import pallas as pl
from jax.experimental.pallas import tpu as pltpu
from jax.sharding import PartitionSpec as P

TOP_BITS = 14
LEAST_TOP = 1e-30
FACTORS = 4
LANES = 128
GROUPS = 2


def matmul(left, right):
    return jnp.dot(left, right, preferred_element_type=jnp.float32)


def times_down(left, w_down):
    return lax.dot_general(
        left, w_down, (((1,), (1,)), ((), ())), preferred_element_type=jnp.float32
    )


def slot_masks(count):
    bits = count.bit_length() - 1
    assert 1 << bits == count
    return [sum(((s >> b) & 1) << (bits - 1 - b) for b in range(bits)) for s in range(count)]


def swap(values, axis, mask):
    count = lax.axis_size(axis)
    return lax.ppermute(values, axis, [(i, i ^ mask) for i in range(count)])


def shift(values, axis, by=1):
    count = lax.axis_size(axis)
    return lax.ppermute(values, axis, [(i, (i + by) % count) for i in range(count)])


def coded(values):
    top = jnp.max(jnp.abs(values), axis=-1, keepdims=True)
    power = jnp.ceil(jnp.log2(jnp.maximum(top, LEAST_TOP))) - TOP_BITS
    factors, left = [], power
    for _ in range(FACTORS):
        factors.append(jnp.clip(left, -14.0, 15.0))
        left = left - factors[-1]
    shape = (*values.shape[:-1], LANES)
    at = lax.broadcasted_iota(jnp.int32, shape, len(shape) - 1) // (LANES // FACTORS)
    factor = factors[0]
    for i in range(1, FACTORS):
        factor = jnp.where(at == i, factors[i], factor)
    body = values * jnp.exp2(left - power)
    return jnp.concatenate([body, jnp.exp2(factor)], axis=-1).astype(jnp.float16)


def decoded(code):
    width = code.shape[-1] - LANES
    values = code[..., :width].astype(jnp.float32)
    for i in range(FACTORS):
        at = width + i * (LANES // FACTORS)
        values = values * code[..., at : at + 1].astype(jnp.float32)
    return values


def tie(values, after):
    return lax.optimization_barrier((values, *after))[0] if after else values


def last_kernel(scale, parts, *refs):
    turned, bars, out_ref = refs[:parts], refs[parts : 2 * parts], refs[2 * parts]
    height = out_ref.shape[0]
    step = 512 if height % 512 == 0 else height

    @pl.loop(0, height // step)
    def _(at):
        rows = pl.ds(pl.multiple_of(at * step, step), step)
        total = jnp.dot(turned[0][rows, :], bars[0][...], preferred_element_type=jnp.float32)
        for left, right in zip(turned[1:], bars[1:]):
            total += jnp.dot(left[rows, :], right[...], preferred_element_type=jnp.float32)
        out_ref[rows, :] = total * scale


def last_product(turned, bars, tokens):
    features, hidden = turned[0].shape[0], bars[0].shape[1]
    tile = 512 if hidden % 512 == 0 else hidden
    depth = sum(t.shape[1] for t in turned)
    return pl.pallas_call(
        functools.partial(last_kernel, 1.0 / tokens, len(turned)),
        grid=(hidden // tile,),
        out_shape=jax.ShapeDtypeStruct((features, hidden), jnp.float32),
        in_specs=[pl.BlockSpec(t.shape, lambda j: (0, 0)) for t in turned]
        + [pl.BlockSpec((b.shape[0], tile), lambda j: (0, j)) for b in bars],
        out_specs=pl.BlockSpec((features, tile), lambda j: (0, j)),
        compiler_params=pltpu.CompilerParams(vmem_limit_bytes=40 * 1024 * 1024),
        cost_estimate=pl.CostEstimate(
            flops=2 * features * hidden * depth,
            bytes_accessed=features * hidden * 4 + depth * (features + hidden) * 2,
            transcendentals=0,
        ),
    )(*turned, *bars)


def per_device(inputs, w_gate, w_up, w_down, query, curvature):
    ring, count = lax.axis_size("row"), lax.axis_size("col")
    assert lax.axis_size("grp") == 2 and ring % GROUPS == 0 and count >= 4
    shard, width = inputs.shape
    tokens = shard * ring
    rows = shard // 2 // count
    per_group = ring // GROUPS
    masks = slot_masks(count)
    place, grp, me = lax.axis_index("col"), lax.axis_index("grp"), lax.axis_index("row")

    def own_rows(array, start, half):
        begin = start + half * (shard // 2)
        return jnp.stack(
            [
                lax.dynamic_slice_in_dim(array, begin + (place ^ mask) * rows, rows, 0)
                for mask in masks
            ]
        )

    def joined(pieces):
        return jnp.concatenate(pieces, axis=1).reshape(-1, pieces[0].shape[-1])

    halves = (grp, 1 - grp)
    own = [own_rows(inputs, 0, half) for half in halves]
    fetched = {(0, 0): own[0], (1, 0): own[1]}
    for k in range(1, ring):
        needed = [fetched[0, i] for i in range(1, per_group)] if k >= per_group else []
        fetched[0, k] = shift(tie(own[0], needed), "row", k)

    def fetch_other(step, after):
        for k in step:
            if k:
                fetched[1, k] = swap(tie(fetched[0, k], after), "grp", 1)
        return [fetched[1, k] for k in step if k]

    gate_scale = 2.0 ** math.floor(math.log2(65504.0 / (0.375 * width * count)))

    def pack(values, form):
        if form == "gate":
            return (values * gate_scale).astype(jnp.float16)
        return coded(values) if form == "up" else values.astype(jnp.bfloat16)

    def unpack(values, form):
        if form == "up":
            return decoded(values)
        values = values.astype(jnp.float32)
        return values * (1.0 / gate_scale) if form == "gate" else values

    def sum_over_col(part, form):
        half = part.shape[0] // 2
        first = part[half:]
        got = swap(first, "col", 1)
        cut = half // 2
        own, give = part[:cut] + got[:cut], part[cut:half] + got[cut:]
        mask, marks = 2, None
        while True:
            sent = pack(give, form)
            got = swap(sent, "col", mask)
            marks = marks or ([first], [sent], [got])
            own = own + unpack(got, form)
            mask *= 2
            if mask >= count:
                return own, *marks
            cut = own.shape[0] // 2
            own, give = own[:cut], own[cut:]

    def gather_over_col(values):
        mask, mark = count // 2, None
        while mask >= 1:
            got = swap(values, "col", mask)
            mark = got if mark is None else mark
            values = jnp.concatenate([values, got], axis=0)
            mask //= 2
        return values, mark

    steps = [list(range(j * per_group, (j + 1) * per_group)) for j in range(GROUPS)]
    last = ring - 1
    sums, marks, xs = {}, [], {}
    gains = [[None] * GROUPS, [None] * GROUPS]
    moved = {}

    def project(half, j, form, after):
        for sent in [mark[1] for mark in marks[-2:-1]] + [mark[2] for mark in marks[-3:-2]]:
            after = after + sent
        if (half, j) in xs:
            x = tie(xs[half, j], after)
        else:
            xs[half, j] = x = joined([tie(fetched[half, k], after) for k in steps[j]])
        weight = {"gate": w_gate, "up": w_up, "tangent": query}[form]
        sums[half, j, form], *mark = sum_over_col(matmul(x, weight), form)
        marks.append(mark)
        return mark[0]

    def hidden_rows(half, j, after):
        if half == 0:
            gate_out, up_out = sums[0, j, "gate"], sums[0, j, "up"]
            sigmas = jax.nn.sigmoid(gate_out)
            gains[0][j] = sigmas * (1.0 + gate_out * (1.0 - sigmas)) * up_out
        tangent = tie(sums[half, j, "tangent"], after)
        hidden = (gains[half][j] * tangent).astype(jnp.bfloat16)
        return gather_over_col(hidden)

    def share_gain(j, after):
        both = lax.all_gather(tie(gains[0][j], after), "grp")
        gains[1][j] = lax.dynamic_index_in_dim(both, 1 - grp, 0, keepdims=False)

    def out_sums(half, j, hidden, after):
        out = matmul(tie(hidden, after), w_down).reshape(count, per_group, rows, width)
        for i, k in enumerate(steps[j]):
            piece = out[:, i]
            if k < last:
                piece = piece.astype(jnp.bfloat16)
                mark = piece
                piece = shift(piece, "row", last - k)
            moved[half, k] = piece
        return mark

    def scaled_pieces(half, after):
        total = moved[half, last]
        for k in range(last):
            total = total + tie(moved[half, k], after).astype(jnp.float32)
        curv = own_rows(curvature, (me + 1) % ring * shard, halves[half])
        pieces = [None] * last + [(curv * total).astype(jnp.bfloat16)]
        cut = ring // 4
        for k in reversed(range(cut, last)):
            pieces[k] = shift(pieces[k + 1], "row", -1)
        piece = tie(pieces[last], [pieces[steps[-1][0]]])
        for k in range(cut):
            pieces[k] = piece = shift(piece, "row")
        return pieces

    turned, bars = [], []

    def back(half, j, pieces, after):
        x = joined([tie(pieces[k], after) for k in steps[j]])
        turned.append(tie(xs[half, j], pieces[last:]).T)
        own, first, sent, got = sum_over_col(times_down(x, w_down), "back")
        whole, near = gather_over_col((own * gains[half][j]).astype(jnp.bfloat16))
        bars.append(whole)
        return first, sent, got, [near]

    tail = GROUPS - 1
    early, others = [], []
    for j in range(GROUPS):
        first = project(0, j, "up", [])
        others.append(fetch_other(steps[j], first))
        if j:
            early.append(hidden_rows(0, j - 1, first))
        project(0, j, "gate", others[0] if j == tail else [])
        first = project(0, j, "tangent", [])
        if j:
            share_gain(j - 1, first)
    ready = [out_sums(0, j, early[j][0], marks[-2][1]) for j in range(tail)]
    first = project(1, 0, "tangent", ready)
    hidden, _ = hidden_rows(0, tail, first)
    for j in range(1, GROUPS):
        first = project(1, j, "tangent", others[j])
    share_gain(tail, first)
    ready = [out_sums(0, tail, hidden, [])]
    pieces = scaled_pieces(0, [])

    hidden = [hidden_rows(1, j, []) for j in range(GROUPS)]
    ready = [out_sums(1, j, hidden[j][0], []) for j in range(tail)]
    first, sent, got, near = back(0, tail, pieces, ready)
    ready = [out_sums(1, tail, hidden[tail][0], sent)]
    others = scaled_pieces(1, near)
    for j in reversed(range(tail)):
        back(0, j, pieces, ready + got + others[last:])
    for j in reversed(range(GROUPS)):
        back(1, j, others, others)
    return last_product(turned, bars, tokens)


def solution(mesh):
    in_specs = (
        P("row", "col"),
        P("col", "row"),
        P("col", "row"),
        P("row", "col"),
        P(("grp", "col"), "row"),
        P("grp", "col"),
    )
    out_specs = P(("grp", "col"), "row")
    return jax.shard_map(
        per_device, mesh=mesh, in_specs=in_specs, out_specs=out_specs, check_vma=False
    )
```

```python
import functools
import math

import jax
import jax.numpy as jnp
from jax import lax
from jax.experimental import pallas as pl
from jax.experimental.pallas import tpu as pltpu
from jax.sharding import PartitionSpec as P

TOP_BITS = 14
LEAST_TOP = 1e-30
FACTORS = 4
LANES = 128
GROUPS = 2


def matmul(left, right):
    return jnp.dot(left, right, preferred_element_type=jnp.float32)


def times_down(left, w_down):
    return lax.dot_general(
        left, w_down, (((1,), (1,)), ((), ())), preferred_element_type=jnp.float32
    )


def slot_masks(count):
    bits = count.bit_length() - 1
    assert 1 << bits == count
    return [sum(((s >> b) & 1) << (bits - 1 - b) for b in range(bits)) for s in range(count)]


def swap(values, axis, mask):
    count = lax.axis_size(axis)
    return lax.ppermute(values, axis, [(i, i ^ mask) for i in range(count)])


def shift(values, axis, by=1):
    count = lax.axis_size(axis)
    return lax.ppermute(values, axis, [(i, (i + by) % count) for i in range(count)])


def coded(values):
    top = jnp.max(jnp.abs(values), axis=-1, keepdims=True)
    power = jnp.ceil(jnp.log2(jnp.maximum(top, LEAST_TOP))) - TOP_BITS
    factors, left = [], power
    for _ in range(FACTORS):
        factors.append(jnp.clip(left, -14.0, 15.0))
        left = left - factors[-1]
    shape = (*values.shape[:-1], LANES)
    at = lax.broadcasted_iota(jnp.int32, shape, len(shape) - 1) // (LANES // FACTORS)
    factor = factors[0]
    for i in range(1, FACTORS):
        factor = jnp.where(at == i, factors[i], factor)
    body = values * jnp.exp2(left - power)
    return jnp.concatenate([body, jnp.exp2(factor)], axis=-1).astype(jnp.float16)


def decoded(code):
    width = code.shape[-1] - LANES
    values = code[..., :width].astype(jnp.float32)
    for i in range(FACTORS):
        at = width + i * (LANES // FACTORS)
        values = values * code[..., at : at + 1].astype(jnp.float32)
    return values


def tie(values, after):
    return lax.optimization_barrier((values, *after))[0] if after else values


def last_kernel(scale, parts, *refs):
    turned, bars, out_ref = refs[:parts], refs[parts : 2 * parts], refs[2 * parts]
    height = out_ref.shape[0]
    step = 512 if height % 512 == 0 else height

    @pl.loop(0, height // step)
    def _(at):
        rows = pl.ds(pl.multiple_of(at * step, step), step)
        total = jnp.dot(turned[0][rows, :], bars[0][...], preferred_element_type=jnp.float32)
        for left, right in zip(turned[1:], bars[1:]):
            total += jnp.dot(left[rows, :], right[...], preferred_element_type=jnp.float32)
        out_ref[rows, :] = total * scale


def last_product(turned, bars, tokens):
    features, hidden = turned[0].shape[0], bars[0].shape[1]
    tile = 512 if hidden % 512 == 0 else hidden
    depth = sum(t.shape[1] for t in turned)
    return pl.pallas_call(
        functools.partial(last_kernel, 1.0 / tokens, len(turned)),
        grid=(hidden // tile,),
        out_shape=jax.ShapeDtypeStruct((features, hidden), jnp.float32),
        in_specs=[pl.BlockSpec(t.shape, lambda j: (0, 0)) for t in turned]
        + [pl.BlockSpec((b.shape[0], tile), lambda j: (0, j)) for b in bars],
        out_specs=pl.BlockSpec((features, tile), lambda j: (0, j)),
        compiler_params=pltpu.CompilerParams(vmem_limit_bytes=40 * 1024 * 1024),
        cost_estimate=pl.CostEstimate(
            flops=2 * features * hidden * depth,
            bytes_accessed=features * hidden * 4 + depth * (features + hidden) * 2,
            transcendentals=0,
        ),
    )(*turned, *bars)


def per_device(inputs, w_gate, w_up, w_down, query, curvature):
    ring, count = lax.axis_size("row"), lax.axis_size("col")
    assert lax.axis_size("grp") == 2 and ring % GROUPS == 0 and count >= 4
    shard, width = inputs.shape
    tokens = shard * ring
    rows = shard // 2 // count
    per_group = ring // GROUPS
    masks = slot_masks(count)
    place, grp, me = lax.axis_index("col"), lax.axis_index("grp"), lax.axis_index("row")

    def own_rows(array, start, half):
        begin = start + half * (shard // 2)
        return jnp.stack(
            [
                lax.dynamic_slice_in_dim(array, begin + (place ^ mask) * rows, rows, 0)
                for mask in masks
            ]
        )

    def joined(pieces):
        return jnp.concatenate(pieces, axis=1).reshape(-1, pieces[0].shape[-1])

    halves = (grp, 1 - grp)
    own = [own_rows(inputs, 0, half) for half in halves]
    fetched = {(0, 0): own[0], (1, 0): own[1]}
    for k in range(1, ring):
        needed = [fetched[0, i] for i in range(1, per_group)] if k >= per_group else []
        fetched[0, k] = shift(tie(own[0], needed), "row", k)

    def fetch_other(step, after):
        for k in step:
            if k:
                fetched[1, k] = swap(tie(fetched[0, k], after), "grp", 1)
        return [fetched[1, k] for k in step if k]

    gate_scale = 2.0 ** math.floor(math.log2(65504.0 / (0.375 * width * count)))

    def pack(values, form):
        if form == "gate":
            return (values * gate_scale).astype(jnp.float16)
        return coded(values) if form == "up" else values.astype(jnp.bfloat16)

    def unpack(values, form):
        if form == "up":
            return decoded(values)
        values = values.astype(jnp.float32)
        return values * (1.0 / gate_scale) if form == "gate" else values

    def sum_over_col(part, form):
        half = part.shape[0] // 2
        first = part[half:]
        got = swap(first, "col", 1)
        cut = half // 2
        own, give = part[:cut] + got[:cut], part[cut:half] + got[cut:]
        mask, marks = 2, None
        while True:
            sent = pack(give, form)
            got = swap(sent, "col", mask)
            marks = marks or ([first], [sent], [got])
            own = own + unpack(got, form)
            mask *= 2
            if mask >= count:
                return own, *marks
            cut = own.shape[0] // 2
            own, give = own[:cut], own[cut:]

    def gather_over_col(values):
        mask, mark = count // 2, None
        while mask >= 1:
            got = swap(values, "col", mask)
            mark = got if mark is None else mark
            values = jnp.concatenate([values, got], axis=0)
            mask //= 2
        return values, mark

    steps = [list(range(j * per_group, (j + 1) * per_group)) for j in range(GROUPS)]
    last = ring - 1
    sums, marks, xs = {}, [], {}
    gains = [[None] * GROUPS, [None] * GROUPS]
    moved = {}

    def project(half, j, form, after):
        for sent in [mark[1] for mark in marks[-2:-1]] + [mark[2] for mark in marks[-3:-2]]:
            after = after + sent
        if (half, j) in xs:
            x = tie(xs[half, j], after)
        else:
            xs[half, j] = x = joined([tie(fetched[half, k], after) for k in steps[j]])
        weight = {"gate": w_gate, "up": w_up, "tangent": query}[form]
        sums[half, j, form], *mark = sum_over_col(matmul(x, weight), form)
        marks.append(mark)
        return mark[0]

    def hidden_rows(half, j, after):
        if half == 0:
            gate_out, up_out = sums[0, j, "gate"], sums[0, j, "up"]
            sigmas = jax.nn.sigmoid(gate_out)
            gains[0][j] = sigmas * (1.0 + gate_out * (1.0 - sigmas)) * up_out
        tangent = tie(sums[half, j, "tangent"], after)
        hidden = (gains[half][j] * tangent).astype(jnp.bfloat16)
        return gather_over_col(hidden)

    def share_gain(j, after):
        both = lax.all_gather(tie(gains[0][j], after), "grp")
        gains[1][j] = lax.dynamic_index_in_dim(both, 1 - grp, 0, keepdims=False)

    def out_sums(half, j, hidden, after):
        out = matmul(tie(hidden, after), w_down).reshape(count, per_group, rows, width)
        for i, k in enumerate(steps[j]):
            piece = out[:, i]
            if k < last:
                piece = piece.astype(jnp.bfloat16)
                mark = piece
                piece = shift(piece, "row", last - k)
            moved[half, k] = piece
        return mark

    def scaled_pieces(half, after):
        total = moved[half, last]
        for k in range(last):
            total = total + tie(moved[half, k], after).astype(jnp.float32)
        curv = own_rows(curvature, (me + 1) % ring * shard, halves[half])
        pieces = [None] * last + [(curv * total).astype(jnp.bfloat16)]
        cut = ring // 4
        for k in reversed(range(cut, last)):
            pieces[k] = shift(pieces[k + 1], "row", -1)
        piece = pieces[last]
        for k in range(cut):
            pieces[k] = piece = shift(piece, "row")
        return pieces

    turned, bars = [], []

    def back(half, j, pieces, after):
        x = joined([tie(pieces[k], after) for k in steps[j]])
        turned.append(tie(xs[half, j], pieces[last:]).T)
        own, first, sent, got = sum_over_col(times_down(x, w_down), "back")
        whole, near = gather_over_col((own * gains[half][j]).astype(jnp.bfloat16))
        bars.append(whole)
        return first, sent, got, [near]

    tail = GROUPS - 1
    early, others = [], []
    for j in range(GROUPS):
        first = project(0, j, "up", [])
        others.append(fetch_other(steps[j], first))
        if j:
            early.append(hidden_rows(0, j - 1, first))
        project(0, j, "gate", others[0] if j == tail else [])
        first = project(0, j, "tangent", [])
        if j:
            share_gain(j - 1, first)
    ready = [out_sums(0, j, early[j][0], marks[-2][1]) for j in range(tail)]
    first = project(1, 0, "tangent", ready)
    hidden, _ = hidden_rows(0, tail, first)
    for j in range(1, GROUPS):
        first = project(1, j, "tangent", others[j])
    share_gain(tail, first)
    ready = [out_sums(0, tail, hidden, [])]
    pieces = scaled_pieces(0, [])

    hidden = [hidden_rows(1, j, []) for j in range(GROUPS)]
    ready = [out_sums(1, j, hidden[j][0], []) for j in range(tail)]
    first, sent, got, near = back(0, tail, pieces, ready + pieces[:1])
    ready = [out_sums(1, tail, hidden[tail][0], sent)]
    others = scaled_pieces(1, near)
    after = ready + got + others[last:]
    for j in reversed(range(tail)):
        _, _, after, near = back(0, j, pieces, after)
    after = after + others[:1]
    for j in reversed(range(GROUPS)):
        _, after, _, _ = back(1, j, others, after)
        after = after + near
    return last_product(turned, bars, tokens)


def solution(mesh):
    in_specs = (
        P("row", "col"),
        P("col", "row"),
        P("col", "row"),
        P("row", "col"),
        P(("grp", "col"), "row"),
        P("grp", "col"),
    )
    out_specs = P(("grp", "col"), "row")
    return jax.shard_map(
        per_device, mesh=mesh, in_specs=in_specs, out_specs=out_specs, check_vma=False
    )
```

```python
import functools
import math

import jax
import jax.numpy as jnp
from jax import lax
from jax.experimental import pallas as pl
from jax.experimental.pallas import tpu as pltpu
from jax.sharding import PartitionSpec as P

TOP_BITS = 14
LEAST_TOP = 1e-30
FACTORS = 4
LANES = 128
GROUPS = 2


def matmul(left, right):
    return jnp.dot(left, right, preferred_element_type=jnp.float32)


def times_down(left, w_down):
    return lax.dot_general(
        left, w_down, (((1,), (1,)), ((), ())), preferred_element_type=jnp.float32
    )


def slot_masks(count):
    bits = count.bit_length() - 1
    assert 1 << bits == count
    return [sum(((s >> b) & 1) << (bits - 1 - b) for b in range(bits)) for s in range(count)]


def swap(values, axis, mask):
    count = lax.axis_size(axis)
    return lax.ppermute(values, axis, [(i, i ^ mask) for i in range(count)])


def shift(values, axis, by=1):
    count = lax.axis_size(axis)
    return lax.ppermute(values, axis, [(i, (i + by) % count) for i in range(count)])


def coded(values):
    top = jnp.max(jnp.abs(values), axis=-1, keepdims=True)
    power = jnp.ceil(jnp.log2(jnp.maximum(top, LEAST_TOP))) - TOP_BITS
    factors, left = [], power
    for _ in range(FACTORS):
        factors.append(jnp.clip(left, -14.0, 15.0))
        left = left - factors[-1]
    shape = (*values.shape[:-1], LANES)
    at = lax.broadcasted_iota(jnp.int32, shape, len(shape) - 1) // (LANES // FACTORS)
    factor = factors[0]
    for i in range(1, FACTORS):
        factor = jnp.where(at == i, factors[i], factor)
    body = values * jnp.exp2(left - power)
    return jnp.concatenate([body, jnp.exp2(factor)], axis=-1).astype(jnp.float16)


def decoded(code):
    width = code.shape[-1] - LANES
    values = code[..., :width].astype(jnp.float32)
    for i in range(FACTORS):
        at = width + i * (LANES // FACTORS)
        values = values * code[..., at : at + 1].astype(jnp.float32)
    return values


def tie(values, after):
    return lax.optimization_barrier((values, *after))[0] if after else values


def last_kernel(scale, parts, *refs):
    turned, bars, out_ref = refs[:parts], refs[parts : 2 * parts], refs[2 * parts]
    height = out_ref.shape[0]
    step = 512 if height % 512 == 0 else height

    @pl.loop(0, height // step)
    def _(at):
        rows = pl.ds(pl.multiple_of(at * step, step), step)
        total = jnp.dot(turned[0][rows, :], bars[0][...], preferred_element_type=jnp.float32)
        for left, right in zip(turned[1:], bars[1:]):
            total += jnp.dot(left[rows, :], right[...], preferred_element_type=jnp.float32)
        out_ref[rows, :] = total * scale


def last_product(turned, bars, tokens):
    features, hidden = turned[0].shape[0], bars[0].shape[1]
    tile = 512 if hidden % 512 == 0 else hidden
    depth = sum(t.shape[1] for t in turned)
    return pl.pallas_call(
        functools.partial(last_kernel, 1.0 / tokens, len(turned)),
        grid=(hidden // tile,),
        out_shape=jax.ShapeDtypeStruct((features, hidden), jnp.float32),
        in_specs=[pl.BlockSpec(t.shape, lambda j: (0, 0)) for t in turned]
        + [pl.BlockSpec((b.shape[0], tile), lambda j: (0, j)) for b in bars],
        out_specs=pl.BlockSpec((features, tile), lambda j: (0, j)),
        compiler_params=pltpu.CompilerParams(vmem_limit_bytes=40 * 1024 * 1024),
        cost_estimate=pl.CostEstimate(
            flops=2 * features * hidden * depth,
            bytes_accessed=features * hidden * 4 + depth * (features + hidden) * 2,
            transcendentals=0,
        ),
    )(*turned, *bars)


def per_device(inputs, w_gate, w_up, w_down, query, curvature):
    ring, count = lax.axis_size("row"), lax.axis_size("col")
    assert lax.axis_size("grp") == 2 and ring % GROUPS == 0 and count >= 4
    shard, width = inputs.shape
    tokens = shard * ring
    rows = shard // 2 // count
    per_group = ring // GROUPS
    masks = slot_masks(count)
    place, grp, me = lax.axis_index("col"), lax.axis_index("grp"), lax.axis_index("row")

    def own_rows(array, start, half):
        begin = start + half * (shard // 2)
        return jnp.stack(
            [
                lax.dynamic_slice_in_dim(array, begin + (place ^ mask) * rows, rows, 0)
                for mask in masks
            ]
        )

    def joined(pieces):
        return jnp.concatenate(pieces, axis=1).reshape(-1, pieces[0].shape[-1])

    halves = (grp, 1 - grp)
    own = [own_rows(inputs, 0, half) for half in halves]
    fetched = {(0, 0): own[0], (1, 0): own[1]}
    for k in range(1, ring):
        needed = [fetched[0, i] for i in range(1, per_group)] if k >= per_group else []
        fetched[0, k] = shift(tie(own[0], needed), "row", k)

    def fetch_other(step, after):
        for k in step:
            if k:
                fetched[1, k] = swap(tie(fetched[0, k], after), "grp", 1)
        return [fetched[1, k] for k in step if k]

    gate_scale = 2.0 ** math.floor(math.log2(65504.0 / (0.375 * width * count)))

    def pack(values, form):
        if form == "gate":
            return (values * gate_scale).astype(jnp.float16)
        return coded(values) if form == "up" else values.astype(jnp.bfloat16)

    def unpack(values, form):
        if form == "up":
            return decoded(values)
        values = values.astype(jnp.float32)
        return values * (1.0 / gate_scale) if form == "gate" else values

    def sum_over_col(part, form):
        half = part.shape[0] // 2
        first = part[half:]
        got = swap(first, "col", 1)
        cut = half // 2
        own, give = part[:cut] + got[:cut], part[cut:half] + got[cut:]
        mask, marks = 2, None
        while True:
            sent = pack(give, form)
            got = swap(sent, "col", mask)
            marks = marks or ([first], [sent], [got])
            own = own + unpack(got, form)
            mask *= 2
            if mask >= count:
                return own, *marks
            cut = own.shape[0] // 2
            own, give = own[:cut], own[cut:]

    def gather_over_col(values):
        mask, mark = count // 2, None
        while mask >= 1:
            got = swap(values, "col", mask)
            mark = got if mark is None else mark
            values = jnp.concatenate([values, got], axis=0)
            mask //= 2
        return values, mark

    steps = [list(range(j * per_group, (j + 1) * per_group)) for j in range(GROUPS)]
    last = ring - 1
    sums, marks, xs = {}, [], {}
    gains = [[None] * GROUPS, [None] * GROUPS]
    moved = {}

    def project(half, j, form, after):
        for sent in [mark[1] for mark in marks[-2:-1]] + [mark[2] for mark in marks[-3:-2]]:
            after = after + sent
        if (half, j) in xs:
            x = tie(xs[half, j], after)
        else:
            xs[half, j] = x = joined([tie(fetched[half, k], after) for k in steps[j]])
        weight = {"gate": w_gate, "up": w_up, "tangent": query}[form]
        sums[half, j, form], *mark = sum_over_col(matmul(x, weight), form)
        marks.append(mark)
        return mark[0]

    def hidden_rows(half, j, after):
        if half == 0:
            gate_out, up_out = sums[0, j, "gate"], sums[0, j, "up"]
            sigmas = jax.nn.sigmoid(gate_out)
            gains[0][j] = sigmas * (1.0 + gate_out * (1.0 - sigmas)) * up_out
        tangent = tie(sums[half, j, "tangent"], after)
        hidden = (gains[half][j] * tangent).astype(jnp.bfloat16)
        return gather_over_col(hidden)

    def share_gain(j, after):
        both = lax.all_gather(tie(gains[0][j], after), "grp")
        gains[1][j] = lax.dynamic_index_in_dim(both, 1 - grp, 0, keepdims=False)

    def out_sums(half, j, hidden, after):
        out = matmul(tie(hidden, after), w_down).reshape(count, per_group, rows, width)
        for i, k in enumerate(steps[j]):
            piece = out[:, i]
            if k < last:
                piece = piece.astype(jnp.bfloat16)
                mark = piece
                piece = shift(piece, "row", last - k)
            moved[half, k] = piece
        return mark

    def scaled_pieces(half, after):
        total = moved[half, last]
        for k in range(last):
            total = total + tie(moved[half, k], after).astype(jnp.float32)
        curv = own_rows(curvature, (me + 1) % ring * shard, halves[half])
        pieces = [None] * last + [(curv * total).astype(jnp.bfloat16)]
        cut = ring // 4
        for k in reversed(range(cut, last)):
            pieces[k] = shift(pieces[k + 1], "row", -1)
        piece = pieces[last]
        for k in range(cut):
            pieces[k] = piece = shift(piece, "row")
        return pieces

    turned, bars = [], []

    def back(half, j, pieces, after):
        x = joined([tie(pieces[k], after) for k in steps[j]])
        turned.append(tie(xs[half, j], pieces[last:]).T)
        own, first, sent, got = sum_over_col(times_down(x, w_down), "back")
        whole, near = gather_over_col((own * gains[half][j]).astype(jnp.bfloat16))
        bars.append(whole)
        return first, sent, got, [near]

    tail = GROUPS - 1
    early, others = [], []
    for j in range(GROUPS):
        first = project(0, j, "up", [])
        others.append(fetch_other(steps[j], first))
        if j:
            early.append(hidden_rows(0, j - 1, first))
        project(0, j, "gate", others[0] if j == tail else [])
        first = project(0, j, "tangent", marks[-1][1] if j == tail else [])
        if j:
            share_gain(j - 1, first)
    ready = [out_sums(0, j, early[j][0], marks[-1][1]) for j in range(tail)]
    first = project(1, 0, "tangent", ready)
    hidden, _ = hidden_rows(0, tail, first)
    for j in range(1, GROUPS):
        first = project(1, j, "tangent", others[j])
    share_gain(tail, first)
    ready = [out_sums(0, tail, hidden, [])]
    pieces = scaled_pieces(0, [])

    hidden = [hidden_rows(1, j, []) for j in range(GROUPS)]
    ready = [out_sums(1, j, hidden[j][0], []) for j in range(tail)]
    first, sent, got, near = back(0, tail, pieces, ready + pieces[:1])
    ready = [out_sums(1, tail, hidden[tail][0], sent + pieces)]
    after = ready + got + [moved[1, k] for j in range(tail) for k in steps[j]]
    for j in reversed(range(tail)):
        _, _, after, nextnear = back(0, j, pieces, after)
    pieces = scaled_pieces(1, near)
    after = after + pieces[:1]
    for j in reversed(range(GROUPS)):
        _, after, _, _ = back(1, j, pieces, after)
        after = after + nextnear
    return last_product(turned, bars, tokens)


def solution(mesh):
    in_specs = (
        P("row", "col"),
        P("col", "row"),
        P("col", "row"),
        P("row", "col"),
        P(("grp", "col"), "row"),
        P("grp", "col"),
    )
    out_specs = P(("grp", "col"), "row")
    return jax.shard_map(
        per_device, mesh=mesh, in_specs=in_specs, out_specs=out_specs, check_vma=False
    )
```

```python
import functools
import math

import jax
import jax.numpy as jnp
from jax import lax
from jax.experimental import pallas as pl
from jax.experimental.pallas import tpu as pltpu
from jax.sharding import PartitionSpec as P

TOP_BITS = 14
LEAST_TOP = 1e-30
FACTORS = 4
LANES = 128
GROUPS = 2


def matmul(left, right):
    return jnp.dot(left, right, preferred_element_type=jnp.float32)


def times_down(left, w_down):
    return lax.dot_general(
        left, w_down, (((1,), (1,)), ((), ())), preferred_element_type=jnp.float32
    )


def slot_masks(count):
    bits = count.bit_length() - 1
    assert 1 << bits == count
    return [sum(((s >> b) & 1) << (bits - 1 - b) for b in range(bits)) for s in range(count)]


def swap(values, axis, mask):
    count = lax.axis_size(axis)
    return lax.ppermute(values, axis, [(i, i ^ mask) for i in range(count)])


def shift(values, axis, by=1):
    count = lax.axis_size(axis)
    return lax.ppermute(values, axis, [(i, (i + by) % count) for i in range(count)])


def coded(values):
    top = jnp.max(jnp.abs(values), axis=-1, keepdims=True)
    power = jnp.ceil(jnp.log2(jnp.maximum(top, LEAST_TOP))) - TOP_BITS
    factors, left = [], power
    for _ in range(FACTORS):
        factors.append(jnp.clip(left, -14.0, 15.0))
        left = left - factors[-1]
    shape = (*values.shape[:-1], LANES)
    at = lax.broadcasted_iota(jnp.int32, shape, len(shape) - 1) // (LANES // FACTORS)
    factor = factors[0]
    for i in range(1, FACTORS):
        factor = jnp.where(at == i, factors[i], factor)
    body = values * jnp.exp2(left - power)
    return jnp.concatenate([body, jnp.exp2(factor)], axis=-1).astype(jnp.float16)


def decoded(code):
    width = code.shape[-1] - LANES
    values = code[..., :width].astype(jnp.float32)
    for i in range(FACTORS):
        at = width + i * (LANES // FACTORS)
        values = values * code[..., at : at + 1].astype(jnp.float32)
    return values


def tie(values, after):
    return lax.optimization_barrier((values, *after))[0] if after else values


def last_kernel(scale, parts, *refs):
    turned, bars, out_ref = refs[:parts], refs[parts : 2 * parts], refs[2 * parts]
    height = out_ref.shape[0]
    step = 512 if height % 512 == 0 else height

    @pl.loop(0, height // step)
    def _(at):
        rows = pl.ds(pl.multiple_of(at * step, step), step)
        total = jnp.dot(turned[0][rows, :], bars[0][...], preferred_element_type=jnp.float32)
        for left, right in zip(turned[1:], bars[1:]):
            total += jnp.dot(left[rows, :], right[...], preferred_element_type=jnp.float32)
        out_ref[rows, :] = total * scale


def last_product(turned, bars, tokens):
    features, hidden = turned[0].shape[0], bars[0].shape[1]
    tile = 512 if hidden % 512 == 0 else hidden
    depth = sum(t.shape[1] for t in turned)
    return pl.pallas_call(
        functools.partial(last_kernel, 1.0 / tokens, len(turned)),
        grid=(hidden // tile,),
        out_shape=jax.ShapeDtypeStruct((features, hidden), jnp.float32),
        in_specs=[pl.BlockSpec(t.shape, lambda j: (0, 0)) for t in turned]
        + [pl.BlockSpec((b.shape[0], tile), lambda j: (0, j)) for b in bars],
        out_specs=pl.BlockSpec((features, tile), lambda j: (0, j)),
        compiler_params=pltpu.CompilerParams(vmem_limit_bytes=40 * 1024 * 1024),
        cost_estimate=pl.CostEstimate(
            flops=2 * features * hidden * depth,
            bytes_accessed=features * hidden * 4 + depth * (features + hidden) * 2,
            transcendentals=0,
        ),
    )(*turned, *bars)


def per_device(inputs, w_gate, w_up, w_down, query, curvature):
    ring, count = lax.axis_size("row"), lax.axis_size("col")
    assert lax.axis_size("grp") == 2 and ring % GROUPS == 0 and count >= 4
    shard, width = inputs.shape
    tokens = shard * ring
    rows = shard // 2 // count
    per_group = ring // GROUPS
    masks = slot_masks(count)
    place, grp, me = lax.axis_index("col"), lax.axis_index("grp"), lax.axis_index("row")

    def own_rows(array, start, half):
        begin = start + half * (shard // 2)
        return jnp.stack(
            [
                lax.dynamic_slice_in_dim(array, begin + (place ^ mask) * rows, rows, 0)
                for mask in masks
            ]
        )

    def joined(pieces):
        return jnp.concatenate(pieces, axis=1).reshape(-1, pieces[0].shape[-1])

    halves = (grp, 1 - grp)
    own = [own_rows(inputs, 0, half) for half in halves]
    fetched = {(0, 0): own[0], (1, 0): own[1]}
    for k in range(1, ring):
        needed = [fetched[0, i] for i in range(1, per_group)] if k >= per_group else []
        fetched[0, k] = shift(tie(own[0], needed), "row", k)

    def fetch_other(step, after):
        for k in step:
            if k:
                fetched[1, k] = swap(tie(fetched[0, k], after), "grp", 1)
        return [fetched[1, k] for k in step if k]

    gate_scale = 2.0 ** math.floor(math.log2(65504.0 / (0.375 * width * count)))

    def pack(values, form):
        if form == "gate":
            return (values * gate_scale).astype(jnp.float16)
        return coded(values) if form == "up" else values.astype(jnp.bfloat16)

    def unpack(values, form):
        if form == "up":
            return decoded(values)
        values = values.astype(jnp.float32)
        return values * (1.0 / gate_scale) if form == "gate" else values

    def sum_over_col(part, form):
        half = part.shape[0] // 2
        first = part[half:]
        got = swap(first, "col", 1)
        cut = half // 2
        own, give = part[:cut] + got[:cut], part[cut:half] + got[cut:]
        mask, marks = 2, None
        while True:
            sent = pack(give, form)
            got = swap(sent, "col", mask)
            marks = marks or ([first], [sent], [got])
            own = own + unpack(got, form)
            mask *= 2
            if mask >= count:
                return own, *marks
            cut = own.shape[0] // 2
            own, give = own[:cut], own[cut:]

    def gather_over_col(values):
        mask, mark = count // 2, None
        while mask >= 1:
            got = swap(values, "col", mask)
            mark = got if mark is None else mark
            values = jnp.concatenate([values, got], axis=0)
            mask //= 2
        return values, mark

    steps = [list(range(j * per_group, (j + 1) * per_group)) for j in range(GROUPS)]
    last = ring - 1
    sums, marks, xs = {}, [], {}
    gains = [[None] * GROUPS, [None] * GROUPS]
    moved = {}

    def project(half, j, form, after):
        for sent in [mark[1] for mark in marks[-2:-1]] + [mark[2] for mark in marks[-3:-2]]:
            after = after + sent
        if (half, j) in xs:
            x = tie(xs[half, j], after)
        else:
            xs[half, j] = x = joined([tie(fetched[half, k], after) for k in steps[j]])
        weight = {"gate": w_gate, "up": w_up, "tangent": query}[form]
        sums[half, j, form], *mark = sum_over_col(matmul(x, weight), form)
        marks.append(mark)
        return mark[0]

    def hidden_rows(half, j, after):
        if half == 0:
            gate_out, up_out = sums[0, j, "gate"], sums[0, j, "up"]
            sigmas = jax.nn.sigmoid(gate_out)
            gains[0][j] = sigmas * (1.0 + gate_out * (1.0 - sigmas)) * up_out
        tangent = tie(sums[half, j, "tangent"], after)
        hidden = (gains[half][j] * tangent).astype(jnp.bfloat16)
        return gather_over_col(hidden)

    def share_gain(j, after):
        both = lax.all_gather(tie(gains[0][j], after), "grp")
        gains[1][j] = lax.dynamic_index_in_dim(both, 1 - grp, 0, keepdims=False)

    def out_sums(half, j, hidden, after):
        out = matmul(tie(hidden, after), w_down).reshape(count, per_group, rows, width)
        for i, k in enumerate(steps[j]):
            piece = out[:, i]
            if k < last:
                piece = piece.astype(jnp.bfloat16)
                mark = piece
                piece = shift(piece, "row", last - k)
            moved[half, k] = piece
        return mark

    def scaled_pieces(half, after):
        total = moved[half, last]
        for k in range(last):
            total = total + tie(moved[half, k], after).astype(jnp.float32)
        curv = own_rows(curvature, (me + 1) % ring * shard, halves[half])
        pieces = [None] * last + [(curv * total).astype(jnp.bfloat16)]
        cut = ring // 4
        for k in reversed(range(cut, last)):
            pieces[k] = shift(pieces[k + 1], "row", -1)
        piece = pieces[last]
        for k in range(cut):
            pieces[k] = piece = shift(piece, "row")
        return pieces

    turned, bars = [], []

    def back(half, j, pieces, after):
        x = joined([tie(pieces[k], after) for k in steps[j]])
        turned.append(tie(xs[half, j], pieces[last:]).T)
        own, first, sent, got = sum_over_col(times_down(x, w_down), "back")
        whole, near = gather_over_col((own * gains[half][j]).astype(jnp.bfloat16))
        bars.append(whole)
        return first, sent, got, [near]

    tail = GROUPS - 1
    early, others = [], []
    for j in range(GROUPS):
        first = project(0, j, "up", [])
        others.append(fetch_other(steps[j], first))
        if j:
            early.append(hidden_rows(0, j - 1, first))
        project(0, j, "gate", others[0] if j == tail else [])
        first = project(0, j, "tangent", [])
        if j:
            share_gain(j - 1, first)
    ready = [out_sums(0, j, early[j][0], marks[-2][1]) for j in range(tail)]
    first = project(1, 0, "tangent", ready)
    hidden, _ = hidden_rows(0, tail, first)
    for j in range(1, GROUPS):
        first = project(1, j, "tangent", others[j])
    share_gain(tail, first)
    ready = [out_sums(0, tail, hidden, [])]
    pieces = scaled_pieces(0, [])

    hidden = [hidden_rows(1, j, []) for j in range(GROUPS)]
    ready = [out_sums(1, j, hidden[j][0], []) for j in range(tail)]
    first, sent, got, near = back(0, tail, pieces, ready + pieces[:1])
    ready = [out_sums(1, tail, hidden[tail][0], sent)]
    others = scaled_pieces(1, near)
    after = ready + got + others[:1]
    for j in reversed(range(tail)):
        first, _, _, _ = back(0, j, pieces, after)
    after = others[:1] + first
    for j in reversed(range(GROUPS)):
        _, _, after, _ = back(1, j, others, after)
    return last_product(turned, bars, tokens)


def solution(mesh):
    in_specs = (
        P("row", "col"),
        P("col", "row"),
        P("col", "row"),
        P("row", "col"),
        P(("grp", "col"), "row"),
        P("grp", "col"),
    )
    out_specs = P(("grp", "col"), "row")
    return jax.shard_map(
        per_device, mesh=mesh, in_specs=in_specs, out_specs=out_specs, check_vma=False
    )
```

```python
import functools
import math

import jax
import jax.numpy as jnp
from jax import lax
from jax.experimental import pallas as pl
from jax.experimental.pallas import tpu as pltpu
from jax.sharding import PartitionSpec as P

TOP_BITS = 14
LEAST_TOP = 1e-30
FACTORS = 4
LANES = 128
GROUPS = 2


def matmul(left, right):
    return jnp.dot(left, right, preferred_element_type=jnp.float32)


def times_down(left, w_down):
    return lax.dot_general(
        left, w_down, (((1,), (1,)), ((), ())), preferred_element_type=jnp.float32
    )


def slot_masks(count):
    bits = count.bit_length() - 1
    assert 1 << bits == count
    return [sum(((s >> b) & 1) << (bits - 1 - b) for b in range(bits)) for s in range(count)]


def swap(values, axis, mask):
    count = lax.axis_size(axis)
    return lax.ppermute(values, axis, [(i, i ^ mask) for i in range(count)])


def shift(values, axis, by=1):
    count = lax.axis_size(axis)
    return lax.ppermute(values, axis, [(i, (i + by) % count) for i in range(count)])


def coded(values):
    top = jnp.max(jnp.abs(values), axis=-1, keepdims=True)
    power = jnp.ceil(jnp.log2(jnp.maximum(top, LEAST_TOP))) - TOP_BITS
    factors, left = [], power
    for _ in range(FACTORS):
        factors.append(jnp.clip(left, -14.0, 15.0))
        left = left - factors[-1]
    shape = (*values.shape[:-1], LANES)
    at = lax.broadcasted_iota(jnp.int32, shape, len(shape) - 1) // (LANES // FACTORS)
    factor = factors[0]
    for i in range(1, FACTORS):
        factor = jnp.where(at == i, factors[i], factor)
    body = values * jnp.exp2(left - power)
    return jnp.concatenate([body, jnp.exp2(factor)], axis=-1).astype(jnp.float16)


def decoded(code):
    width = code.shape[-1] - LANES
    values = code[..., :width].astype(jnp.float32)
    for i in range(FACTORS):
        at = width + i * (LANES // FACTORS)
        values = values * code[..., at : at + 1].astype(jnp.float32)
    return values


def tie(values, after):
    return lax.optimization_barrier((values, *after))[0] if after else values


def last_kernel(scale, parts, *refs):
    turned, bars, out_ref = refs[:parts], refs[parts : 2 * parts], refs[2 * parts]
    height = out_ref.shape[0]
    step = 512 if height % 512 == 0 else height

    @pl.loop(0, height // step)
    def _(at):
        rows = pl.ds(pl.multiple_of(at * step, step), step)
        total = jnp.dot(turned[0][rows, :], bars[0][...], preferred_element_type=jnp.float32)
        for left, right in zip(turned[1:], bars[1:]):
            total += jnp.dot(left[rows, :], right[...], preferred_element_type=jnp.float32)
        out_ref[rows, :] = total * scale


def last_product(turned, bars, tokens):
    features, hidden = turned[0].shape[0], bars[0].shape[1]
    tile = 512 if hidden % 512 == 0 else hidden
    depth = sum(t.shape[1] for t in turned)
    return pl.pallas_call(
        functools.partial(last_kernel, 1.0 / tokens, len(turned)),
        grid=(hidden // tile,),
        out_shape=jax.ShapeDtypeStruct((features, hidden), jnp.float32),
        in_specs=[pl.BlockSpec(t.shape, lambda j: (0, 0)) for t in turned]
        + [pl.BlockSpec((b.shape[0], tile), lambda j: (0, j)) for b in bars],
        out_specs=pl.BlockSpec((features, tile), lambda j: (0, j)),
        compiler_params=pltpu.CompilerParams(vmem_limit_bytes=40 * 1024 * 1024),
        cost_estimate=pl.CostEstimate(
            flops=2 * features * hidden * depth,
            bytes_accessed=features * hidden * 4 + depth * (features + hidden) * 2,
            transcendentals=0,
        ),
    )(*turned, *bars)


def per_device(inputs, w_gate, w_up, w_down, query, curvature):
    ring, count = lax.axis_size("row"), lax.axis_size("col")
    assert lax.axis_size("grp") == 2 and ring % GROUPS == 0 and count >= 4
    shard, width = inputs.shape
    tokens = shard * ring
    rows = shard // 2 // count
    per_group = ring // GROUPS
    masks = slot_masks(count)
    place, grp, me = lax.axis_index("col"), lax.axis_index("grp"), lax.axis_index("row")

    def own_rows(array, start, half):
        begin = start + half * (shard // 2)
        return jnp.stack(
            [
                lax.dynamic_slice_in_dim(array, begin + (place ^ mask) * rows, rows, 0)
                for mask in masks
            ]
        )

    def joined(pieces):
        return jnp.concatenate(pieces, axis=1).reshape(-1, pieces[0].shape[-1])

    halves = (grp, 1 - grp)
    own = [own_rows(inputs, 0, half) for half in halves]
    fetched = {(0, 0): own[0], (1, 0): own[1]}
    for k in range(1, ring):
        needed = [fetched[0, i] for i in range(1, per_group)] if k >= per_group else []
        fetched[0, k] = shift(tie(own[0], needed), "row", k)

    def fetch_other(step, after):
        for k in step:
            if k:
                fetched[1, k] = swap(tie(fetched[0, k], after), "grp", 1)
        return [fetched[1, k] for k in step if k]

    gate_scale = 2.0 ** math.floor(math.log2(65504.0 / (0.375 * width * count)))

    def pack(values, form):
        if form == "gate":
            return (values * gate_scale).astype(jnp.float16)
        return coded(values) if form == "up" else values.astype(jnp.bfloat16)

    def unpack(values, form):
        if form == "up":
            return decoded(values)
        values = values.astype(jnp.float32)
        return values * (1.0 / gate_scale) if form == "gate" else values

    def sum_over_col(part, form):
        half = part.shape[0] // 2
        first = part[half:]
        got = swap(first, "col", 1)
        cut = half // 2
        own, give = part[:cut] + got[:cut], part[cut:half] + got[cut:]
        mask, marks = 2, None
        while True:
            sent = pack(give, form)
            got = swap(sent, "col", mask)
            marks = marks or ([first], [sent], [got])
            own = own + unpack(got, form)
            mask *= 2
            if mask >= count:
                return own, *marks
            cut = own.shape[0] // 2
            own, give = own[:cut], own[cut:]

    def gather_over_col(values):
        mask, mark = count // 2, None
        while mask >= 1:
            got = swap(values, "col", mask)
            mark = got if mark is None else mark
            values = jnp.concatenate([values, got], axis=0)
            mask //= 2
        return values, mark

    steps = [list(range(j * per_group, (j + 1) * per_group)) for j in range(GROUPS)]
    last = ring - 1
    sums, marks, xs = {}, [], {}
    gains = [[None] * GROUPS, [None] * GROUPS]
    moved = {}

    def project(half, j, form, after):
        for sent in [mark[1] for mark in marks[-2:-1]] + [mark[2] for mark in marks[-3:-2]]:
            after = after + sent
        if (half, j) in xs:
            x = tie(xs[half, j], after)
        else:
            xs[half, j] = x = joined([tie(fetched[half, k], after) for k in steps[j]])
        weight = {"gate": w_gate, "up": w_up, "tangent": query}[form]
        sums[half, j, form], *mark = sum_over_col(matmul(x, weight), form)
        marks.append(mark)
        return mark[0]

    def hidden_rows(half, j, after):
        if half == 0:
            gate_out, up_out = sums[0, j, "gate"], sums[0, j, "up"]
            sigmas = jax.nn.sigmoid(gate_out)
            gains[0][j] = sigmas * (1.0 + gate_out * (1.0 - sigmas)) * up_out
        tangent = tie(sums[half, j, "tangent"], after)
        hidden = (gains[half][j] * tangent).astype(jnp.bfloat16)
        return gather_over_col(hidden)

    def share_gain(j, after):
        both = lax.all_gather(tie(gains[0][j], after), "grp")
        gains[1][j] = lax.dynamic_index_in_dim(both, 1 - grp, 0, keepdims=False)

    def out_sums(half, j, hidden, after):
        out = matmul(tie(hidden, after), w_down).reshape(count, per_group, rows, width)
        for i, k in enumerate(steps[j]):
            piece = out[:, i]
            if k < last:
                piece = piece.astype(jnp.bfloat16)
                mark = piece
                piece = shift(piece, "row", last - k)
            moved[half, k] = piece
        return mark

    def scaled_pieces(half, after):
        total = moved[half, last]
        for k in range(last):
            total = total + tie(moved[half, k], after).astype(jnp.float32)
        curv = own_rows(curvature, (me + 1) % ring * shard, halves[half])
        pieces = [None] * last + [(curv * total).astype(jnp.bfloat16)]
        cut = ring // 4
        for k in reversed(range(cut, last)):
            pieces[k] = shift(pieces[k + 1], "row", -1)
        piece = pieces[last]
        for k in range(cut):
            pieces[k] = piece = shift(piece, "row")
        return pieces

    turned, bars = [], []

    def back(half, j, pieces, after):
        x = joined([tie(pieces[k], after) for k in steps[j]])
        turned.append(tie(xs[half, j], pieces[last:]).T)
        own, first, sent, got = sum_over_col(times_down(x, w_down), "back")
        whole, near = gather_over_col((own * gains[half][j]).astype(jnp.bfloat16))
        bars.append(whole)
        return first, sent, got, [near]

    tail = GROUPS - 1
    early, others = [], []
    for j in range(GROUPS):
        first = project(0, j, "up", [])
        others.append(fetch_other(steps[j], first))
        if j:
            early.append(hidden_rows(0, j - 1, first))
        project(0, j, "gate", others[0] if j == tail else [])
        first = project(0, j, "tangent", [])
        if j:
            share_gain(j - 1, first)
    ready = [out_sums(0, j, early[j][0], marks[-2][1]) for j in range(tail)]
    first = project(1, 0, "tangent", ready)
    hidden, _ = hidden_rows(0, tail, first)
    for j in range(1, GROUPS):
        first = project(1, j, "tangent", others[j])
    share_gain(tail, first)
    ready = [out_sums(0, tail, hidden, [])]
    pieces = scaled_pieces(0, [])

    hidden = [hidden_rows(1, j, []) for j in range(GROUPS)]
    ready = [out_sums(1, j, hidden[j][0], []) for j in range(tail)]
    first, sent, got, near = back(0, tail, pieces, ready + pieces[:1])
    ready = [out_sums(1, tail, hidden[tail][0], sent)]
    others = scaled_pieces(1, near)
    after = ready + got + others[last:]
    for j in reversed(range(tail)):
        _, _, after, near = back(0, j, pieces, after)
    after = after + others[:1]
    for j in reversed(range(GROUPS)):
        _, _, after, _ = back(1, j, others, after)
        after = after + near
    return last_product(turned, bars, tokens)


def solution(mesh):
    in_specs = (
        P("row", "col"),
        P("col", "row"),
        P("col", "row"),
        P("row", "col"),
        P(("grp", "col"), "row"),
        P("grp", "col"),
    )
    out_specs = P(("grp", "col"), "row")
    return jax.shard_map(
        per_device, mesh=mesh, in_specs=in_specs, out_specs=out_specs, check_vma=False
    )
```

```python
import functools
import math

import jax
import jax.numpy as jnp
from jax import lax
from jax.experimental import pallas as pl
from jax.experimental.pallas import tpu as pltpu
from jax.sharding import PartitionSpec as P

TOP_BITS = 14
LEAST_TOP = 1e-30
FACTORS = 4
LANES = 128
GROUPS = 2


def matmul(left, right):
    return jnp.dot(left, right, preferred_element_type=jnp.float32)


def times_down(left, w_down):
    return lax.dot_general(
        left, w_down, (((1,), (1,)), ((), ())), preferred_element_type=jnp.float32
    )


def slot_masks(count):
    bits = count.bit_length() - 1
    assert 1 << bits == count
    return [sum(((s >> b) & 1) << (bits - 1 - b) for b in range(bits)) for s in range(count)]


def swap(values, axis, mask):
    count = lax.axis_size(axis)
    return lax.ppermute(values, axis, [(i, i ^ mask) for i in range(count)])


def shift(values, axis, by=1):
    count = lax.axis_size(axis)
    return lax.ppermute(values, axis, [(i, (i + by) % count) for i in range(count)])


def coded(values):
    top = jnp.max(jnp.abs(values), axis=-1, keepdims=True)
    power = jnp.ceil(jnp.log2(jnp.maximum(top, LEAST_TOP))) - TOP_BITS
    factors, left = [], power
    for _ in range(FACTORS):
        factors.append(jnp.clip(left, -14.0, 15.0))
        left = left - factors[-1]
    shape = (*values.shape[:-1], LANES)
    at = lax.broadcasted_iota(jnp.int32, shape, len(shape) - 1) // (LANES // FACTORS)
    factor = factors[0]
    for i in range(1, FACTORS):
        factor = jnp.where(at == i, factors[i], factor)
    body = values * jnp.exp2(left - power)
    return jnp.concatenate([body, jnp.exp2(factor)], axis=-1).astype(jnp.float16)


def decoded(code):
    width = code.shape[-1] - LANES
    values = code[..., :width].astype(jnp.float32)
    for i in range(FACTORS):
        at = width + i * (LANES // FACTORS)
        values = values * code[..., at : at + 1].astype(jnp.float32)
    return values


def tie(values, after):
    return lax.optimization_barrier((values, *after))[0] if after else values


def last_kernel(scale, parts, *refs):
    turned, bars, out_ref = refs[:parts], refs[parts : 2 * parts], refs[2 * parts]
    height = out_ref.shape[0]
    step = 512 if height % 512 == 0 else height

    @pl.loop(0, height // step)
    def _(at):
        rows = pl.ds(pl.multiple_of(at * step, step), step)
        total = jnp.dot(turned[0][rows, :], bars[0][...], preferred_element_type=jnp.float32)
        for left, right in zip(turned[1:], bars[1:]):
            total += jnp.dot(left[rows, :], right[...], preferred_element_type=jnp.float32)
        out_ref[rows, :] = total * scale


def last_product(turned, bars, tokens):
    features, hidden = turned[0].shape[0], bars[0].shape[1]
    tile = 512 if hidden % 512 == 0 else hidden
    depth = sum(t.shape[1] for t in turned)
    return pl.pallas_call(
        functools.partial(last_kernel, 1.0 / tokens, len(turned)),
        grid=(hidden // tile,),
        out_shape=jax.ShapeDtypeStruct((features, hidden), jnp.float32),
        in_specs=[pl.BlockSpec(t.shape, lambda j: (0, 0)) for t in turned]
        + [pl.BlockSpec((b.shape[0], tile), lambda j: (0, j)) for b in bars],
        out_specs=pl.BlockSpec((features, tile), lambda j: (0, j)),
        compiler_params=pltpu.CompilerParams(vmem_limit_bytes=40 * 1024 * 1024),
        cost_estimate=pl.CostEstimate(
            flops=2 * features * hidden * depth,
            bytes_accessed=features * hidden * 4 + depth * (features + hidden) * 2,
            transcendentals=0,
        ),
    )(*turned, *bars)


def per_device(inputs, w_gate, w_up, w_down, query, curvature):
    ring, count = lax.axis_size("row"), lax.axis_size("col")
    assert lax.axis_size("grp") == 2 and ring % GROUPS == 0 and count >= 4
    shard, width = inputs.shape
    tokens = shard * ring
    rows = shard // 2 // count
    per_group = ring // GROUPS
    masks = slot_masks(count)
    place, grp, me = lax.axis_index("col"), lax.axis_index("grp"), lax.axis_index("row")

    def own_rows(array, start, half):
        begin = start + half * (shard // 2)
        return jnp.stack(
            [
                lax.dynamic_slice_in_dim(array, begin + (place ^ mask) * rows, rows, 0)
                for mask in masks
            ]
        )

    def joined(pieces):
        return jnp.concatenate(pieces, axis=1).reshape(-1, pieces[0].shape[-1])

    halves = (grp, 1 - grp)
    own = [own_rows(inputs, 0, half) for half in halves]
    fetched = {(0, 0): own[0], (1, 0): own[1]}
    for k in range(1, ring):
        needed = [fetched[0, i] for i in range(1, per_group)] if k >= per_group else []
        fetched[0, k] = shift(tie(own[0], needed), "row", k)

    def fetch_other(step, after):
        for k in step:
            if k:
                fetched[1, k] = swap(tie(fetched[0, k], after), "grp", 1)
        return [fetched[1, k] for k in step if k]

    gate_scale = 2.0 ** math.floor(math.log2(65504.0 / (0.375 * width * count)))

    def pack(values, form):
        if form == "gate":
            return (values * gate_scale).astype(jnp.float16)
        return coded(values) if form == "up" else values.astype(jnp.bfloat16)

    def unpack(values, form):
        if form == "up":
            return decoded(values)
        values = values.astype(jnp.float32)
        return values * (1.0 / gate_scale) if form == "gate" else values

    def sum_over_col(part, form):
        half = part.shape[0] // 2
        first = part[half:]
        got = swap(first, "col", 1)
        cut = half // 2
        own, give = part[:cut] + got[:cut], part[cut:half] + got[cut:]
        mask, marks = 2, None
        while True:
            sent = pack(give, form)
            got = swap(sent, "col", mask)
            marks = marks or ([first], [sent], [got])
            own = own + unpack(got, form)
            mask *= 2
            if mask >= count:
                return own, *marks
            cut = own.shape[0] // 2
            own, give = own[:cut], own[cut:]

    def gather_over_col(values):
        mask, mark = count // 2, None
        while mask >= 1:
            got = swap(values, "col", mask)
            mark = got if mark is None else mark
            values = jnp.concatenate([values, got], axis=0)
            mask //= 2
        return values, mark

    steps = [list(range(j * per_group, (j + 1) * per_group)) for j in range(GROUPS)]
    last = ring - 1
    sums, marks, xs = {}, [], {}
    gains = [[None] * GROUPS, [None] * GROUPS]
    moved = {}

    def project(half, j, form, after):
        for sent in [mark[1] for mark in marks[-2:-1]] + [mark[2] for mark in marks[-3:-2]]:
            after = after + sent
        if (half, j) in xs:
            x = tie(xs[half, j], after)
        else:
            xs[half, j] = x = joined([tie(fetched[half, k], after) for k in steps[j]])
        weight = {"gate": w_gate, "up": w_up, "tangent": query}[form]
        sums[half, j, form], *mark = sum_over_col(matmul(x, weight), form)
        marks.append(mark)
        return mark[0]

    def hidden_rows(half, j, after):
        if half == 0:
            gate_out, up_out = sums[0, j, "gate"], sums[0, j, "up"]
            sigmas = jax.nn.sigmoid(gate_out)
            gains[0][j] = sigmas * (1.0 + gate_out * (1.0 - sigmas)) * up_out
        tangent = tie(sums[half, j, "tangent"], after)
        hidden = (gains[half][j] * tangent).astype(jnp.bfloat16)
        return gather_over_col(hidden)

    def share_gain(j, after):
        both = lax.all_gather(tie(gains[0][j], after), "grp")
        gains[1][j] = lax.dynamic_index_in_dim(both, 1 - grp, 0, keepdims=False)

    def out_sums(half, j, hidden, after):
        out = matmul(tie(hidden, after), w_down).reshape(count, per_group, rows, width)
        for i, k in enumerate(steps[j]):
            piece = out[:, i]
            if k < last:
                piece = piece.astype(jnp.bfloat16)
                mark = piece
                piece = shift(piece, "row", last - k)
            moved[half, k] = piece
        return mark

    def scaled_pieces(half, after):
        total = moved[half, last]
        for k in range(last):
            total = total + tie(moved[half, k], after).astype(jnp.float32)
        curv = own_rows(curvature, (me + 1) % ring * shard, halves[half])
        pieces = [None] * last + [(curv * total).astype(jnp.bfloat16)]
        cut = ring // 4
        for k in reversed(range(cut, last)):
            pieces[k] = shift(pieces[k + 1], "row", -1)
        piece = pieces[last]
        for k in range(cut):
            pieces[k] = piece = shift(piece, "row")
        return pieces

    turned, bars = [], []

    def back(half, j, pieces, after):
        x = joined([tie(pieces[k], after) for k in steps[j]])
        turned.append(tie(xs[half, j], pieces[last:]).T)
        own, first, sent, got = sum_over_col(times_down(x, w_down), "back")
        whole, near = gather_over_col((own * gains[half][j]).astype(jnp.bfloat16))
        bars.append(whole)
        return first, sent, got, [near]

    tail = GROUPS - 1
    early, others = [], []
    for j in range(GROUPS):
        first = project(0, j, "up", [])
        others.append(fetch_other(steps[j], first))
        if j:
            early.append(hidden_rows(0, j - 1, first))
        project(0, j, "gate", others[0] if j == tail else [])
        first = project(0, j, "tangent", [])
        if j:
            share_gain(j - 1, first)
    ready = [out_sums(0, j, early[j][0], marks[-2][1]) for j in range(tail)]
    first = project(1, 0, "tangent", ready)
    hidden, _ = hidden_rows(0, tail, first)
    for j in range(1, GROUPS):
        first = project(1, j, "tangent", others[j])
    share_gain(tail, first)
    ready = [out_sums(0, tail, hidden, [])]
    pieces = scaled_pieces(0, [])

    hidden = [hidden_rows(1, j, []) for j in range(GROUPS)]
    ready = [out_sums(1, j, hidden[j][0], []) for j in range(tail)]
    first, sent, got, near = back(0, tail, pieces, ready + pieces[:1])
    ready = [out_sums(1, tail, hidden[tail][0], sent)]
    others = scaled_pieces(1, near)
    after = ready + got + others[last:]
    for j in reversed(range(tail)):
        _, _, after, near = back(0, j, pieces, after)
    after = after + others[:1]
    for j in reversed(range(GROUPS)):
        _, after, _, _ = back(1, j, others, after + turned)
        after = after + near
    return last_product(turned, bars, tokens)


def solution(mesh):
    in_specs = (
        P("row", "col"),
        P("col", "row"),
        P("col", "row"),
        P("row", "col"),
        P(("grp", "col"), "row"),
        P("grp", "col"),
    )
    out_specs = P(("grp", "col"), "row")
    return jax.shard_map(
        per_device, mesh=mesh, in_specs=in_specs, out_specs=out_specs, check_vma=False
    )
```
